32 devices in a mesh: az: 8 (over y, x, core), rad: 4 (over z).
Axes of the slice: x: 2, y: 2, z: 4, core: 2. Of those that a mesh axis runs over, the one named last changes fastest.
Arguments:
- density: float32 [4, 128, 512], P(None, 'az', 'rad'), may hold values from 1 to 2
- momentum: float32 [3, 4, 128, 512], P(None, None, 'az', 'rad'), may hold values from -2.5 to 2.5
- magnetic: float32 [3, 4, 128, 512], P(None, None, 'az', 'rad'), may hold values from -3 to 3
- tracer: float32 [4, 128, 512], P(None, 'az', 'rad'), may hold values from 0 to 1
- shear_offset: int32 [2], replicated, may hold values from 0 to 79, as said below
Outputs:
- new_state: float32 [8, 4, 128, 512], P(None, None, 'az', 'rad')
The draws below stay inside these ranges and needn't reach their ends.
Inputs may be any that keep to these rules, and one draw needn't show every extreme that they name: shear_offset[0] is below 16; shear_offset[1] is 64 plus a whole number below 16.
All inputs are finite; a program needn't handle non-finite values.
Results may differ from the reference program's by a relative error of at most 0.00002.
Values sent between devices are 32-bit elements; how exact they have to be, the bound alone decides.
No kernel may reach another device: no remote copies, remote signals or barrier semaphores. Data moves between devices by JAX's collectives and lax.ppermute only.
A program may use at most 64 MiB of HBM per device.

```python
import jax
import jax.numpy as jnp
from jax import lax

NZ = 4
AZ_DEV = 16
NY = 128
NX = 512


def draw_shear_offset(key, part):
    first_key = jax.random.fold_in(key, 11)
    second_key = jax.random.fold_in(key, 23)
    first = jax.random.randint(first_key, (1,), 0, AZ_DEV, dtype=jnp.int32)
    second = jax.random.randint(second_key, (1,), 0, AZ_DEV, dtype=jnp.int32) + NY // 2
    return jnp.concatenate([first, second]).astype(jnp.int32)


def shard_levels(rng, shape, cuts, smallest, top_value):
    loudness = 1.0
    for position, shards_of in cuts:
        steps = jax.random.uniform(jax.random.fold_in(jax.random.fold_in(rng, 6), position), (shards_of,), jnp.float32, smallest / len(cuts), top_value / len(cuts))
        loudness = loudness * jnp.repeat(jnp.exp(steps), shape[position] // shards_of).reshape((-1,) + (1,) * (len(shape) - 1 - position))
    return loudness


def bell_draw(stream_key, dims, width, reach, pieces=(), held_as=jnp.bfloat16):
    loudness = shard_levels(stream_key, dims, pieces, -0.22, 0.18) if pieces else 1.0
    values = jax.random.normal(stream_key, dims, jnp.float32) * width * loudness
    return jnp.minimum(jnp.maximum(values, -reach), reach).astype(held_as)


def setup_inputs(seed: int = 0) -> dict:
    key_of = jax.random.split(jax.random.key(seed), 6)
    density = jnp.clip(1.0 + 1.0 * jax.random.uniform(key_of[0], (NZ, NY, NX), jnp.float32) ** shard_levels(key_of[0], (NZ, NY, NX), ((1, 8), (2, 4)), -0.2, 0.2), 1.0, 2.0)
    momentum = bell_draw(key_of[1], (3, NZ, NY, NX), 0.4, 2.5, ((2, 8), (3, 4)), jnp.float32)
    magnetic = bell_draw(key_of[2], (3, NZ, NY, NX), 0.8, 3.0, ((2, 8), (3, 4)), jnp.float32)
    tracer = jnp.clip(1.0 * jax.random.uniform(key_of[3], (NZ, NY, NX), jnp.float32) ** shard_levels(key_of[3], (NZ, NY, NX), ((1, 8), (2, 4)), -0.2, 0.2), 0.0, 1.0)
    shear_offset = draw_shear_offset(jax.random.fold_in(key_of[5], 71), 0)
    return {"density": density, "momentum": momentum, "magnetic": magnetic, "tracer": tracer, "shear_offset": shear_offset}


time_step = 0.025
viscosity = 0.5
sound_squared = 1.0
shear_speed = 1.0
frac_weight = 0.375


def fluxes(padded, direction):
    density_part = padded[0]
    velocity = [padded[1 + component] / density_part for component in range(3)]
    field_part = [padded[4 + component] for component in range(3)]
    pressure = sound_squared * density_part + 0.5 * (field_part[0] * field_part[0] + field_part[1] * field_part[1] + field_part[2] * field_part[2])
    normal_vel = velocity[direction]
    normal_mag = field_part[direction]
    result = [padded[1 + direction]]
    for component in range(3):
        summand = padded[1 + component] * normal_vel - field_part[component] * normal_mag
        if component == direction:
            summand = summand + pressure
        result.append(summand)
    for component in range(3):
        result.append(normal_vel * field_part[component] - normal_mag * velocity[component])
    result.append(padded[7] * normal_vel)
    return jnp.stack(result)


def offset_slice(padded, along, length, shift_by):
    return lax.slice_in_dim(padded, 3 + shift_by, 3 + shift_by + length, axis=along)


def central(padded, along, length):
    return (45.0 * (offset_slice(padded, along, length, 1) - offset_slice(padded, along, length, -1))
            - 9.0 * (offset_slice(padded, along, length, 2) - offset_slice(padded, along, length, -2))
            + (offset_slice(padded, along, length, 3) - offset_slice(padded, along, length, -3))) / 60.0


def second(padded, along, length):
    return offset_slice(padded, along, length, 1) - 2.0 * offset_slice(padded, along, length, 0) + offset_slice(padded, along, length, -1)


def tendency(row_padded, col_padded):
    row_count = row_padded.shape[2] - 6
    col_count = col_padded.shape[3] - 6
    core_rows = row_padded[:, :, 3:3 + row_count]
    vertical_pad = jnp.concatenate([core_rows[:, -3:], core_rows, core_rows[:, :3]], axis=1)
    layer_count = core_rows.shape[1]
    summed = -(central(fluxes(col_padded, 0), 3, col_count) + central(fluxes(row_padded, 1), 2, row_count)
               + central(fluxes(vertical_pad, 2), 1, layer_count))
    summed = summed + viscosity * (second(col_padded, 3, col_count) + second(row_padded, 2, row_count)
                                   + second(vertical_pad, 1, layer_count))
    return summed


def blend_rows(window, row_count, lead_weight, trail_weight, jump_sign):
    blended = lead_weight * window[:, :, :row_count] + trail_weight * window[:, :, 1:row_count + 1]
    return jnp.concatenate([blended[:2], blended[2:3] + jump_sign * shear_speed * blended[0:1], blended[3:]], axis=0)


def global_tendency(conserved, offset):
    offset = offset.astype(jnp.int32)
    inner_src = conserved[..., NX - 3:]
    outer_src = conserved[..., :3]
    inner_win = lax.dynamic_slice_in_dim(jnp.concatenate([inner_src, inner_src], axis=2), offset, NY + 1, 2)
    outer_start = (NY - 1 - offset).astype(jnp.int32)
    outer_win = lax.dynamic_slice_in_dim(jnp.concatenate([outer_src, outer_src], axis=2), outer_start, NY + 1, 2)
    inner_ghost = blend_rows(inner_win, NY, 1.0 - frac_weight, frac_weight, 1.0)
    outer_ghost = blend_rows(outer_win, NY, frac_weight, 1.0 - frac_weight, -1.0)
    col_padded = jnp.concatenate([inner_ghost, conserved, outer_ghost], axis=3)
    row_padded = jnp.concatenate([conserved[:, :, -3:], conserved, conserved[:, :, :3]], axis=2)
    return tendency(row_padded, col_padded)


def reference(density, momentum, magnetic, tracer, shear_offset):
    conserved = jnp.concatenate([density[None], momentum, magnetic, tracer[None]], axis=0)
    section_one = conserved + time_step * global_tendency(conserved, shear_offset[0])
    return 0.5 * conserved + 0.5 * (section_one + time_step * global_tendency(section_one, shear_offset[1]))
```

```python
import functools

import jax
import jax.numpy as jnp
from jax import lax
from jax.experimental import pallas as pl
from jax.experimental.pallas import tpu as pltpu
from jax.sharding import PartitionSpec as P

time_step = 0.025
viscosity = 0.5
sound_squared = 1.0
shear_speed = 1.0
frac_weight = 0.375
stencil = ((1, 45.0 / 60.0), (2, -9.0 / 60.0), (3, 1.0 / 60.0))
REACH = 3
FIELDS = 8
SUB = 8
RIGHT = 16
PACK = 8


def struct(*shape):
    return jax.ShapeDtypeStruct(shape, jnp.float32)


def lanes_of(shape):
    return lax.broadcasted_iota(jnp.int32, shape, len(shape) - 1)


def move(values, by):
    count = values.shape[-1]
    if isinstance(by, int):
        by = by % count
        return values if by == 0 else pltpu.roll(values, by, values.ndim - 1)
    return pltpu.roll(values, lax.rem(by + count, count), values.ndim - 1)


def primitives(cells):
    inverse = 1.0 / cells[0]
    velocity = [cells[1 + i] * inverse for i in range(3)]
    squares = cells[4] * cells[4] + cells[5] * cells[5] + cells[6] * cells[6]
    return velocity, sound_squared * cells[0] + 0.5 * squares


def flux(cells, velocity, pressure, direction):
    speed, normal = velocity[direction], cells[4 + direction]
    result = [cells[1 + direction]]
    for i in range(3):
        term = cells[1 + i] * speed - cells[4 + i] * normal
        result.append(term + pressure if i == direction else term)
    for i in range(3):
        result.append(None if i == direction else speed * cells[4 + i] - normal * velocity[i])
    result.append(cells[7] * speed)
    return result


def along_lanes(values, flows, lane, halo_values=None, halo_flows=None):
    count = values.shape[-1]

    def ends(array, halo, width):
        if halo is None:
            return array, array
        return jnp.where(lane < width, halo, array), jnp.where(lane >= count - width, halo, array)

    above, below = ends(values, halo_values, 1)
    up, down = viscosity * above, viscosity * below
    if flows is None:
        return move(up, -1) + move(down, 1)
    total = None
    for distance, weight in stencil:
        above, below = ends(flows, halo_flows, distance)
        plus, minus = -weight * above, weight * below
        if distance == 1:
            plus, minus = plus + up, minus + down
        pair = move(plus, -distance) + move(minus, distance)
        total = pair if total is None else total + pair
    return total


def layer_weights(layers):
    folded = {}
    for distance, weight in stencil:
        for signed, share in ((distance, weight), (-distance, -weight)):
            folded[signed % layers] = folded.get(signed % layers, 0.0) + share
    return {distance: weight for distance, weight in folded.items() if weight != 0.0 and distance != 0}


def strip_section(cells, flows_ref, cells_ref, layers):
    rows, count = cells[0].shape
    slot = count // layers
    velocity, pressure = primitives(cells)
    flow_x, flow_y, flow_z = (flux(cells, velocity, pressure, d) for d in range(3))
    weights = layer_weights(layers)
    result = []
    for f in range(FIELDS):
        total = along_lanes(cells[f], flow_x[f], None)
        total = total + viscosity * (move(cells[f], slot) + move(cells[f], -slot))
        if flow_z[f] is not None:
            for distance, weight in weights.items():
                total = total - weight * move(flow_z[f], -distance * slot)
        cells_ref[SUB : SUB + rows] = cells[f]
        total = total + viscosity * (cells_ref[SUB - 1 : SUB - 1 + rows] + cells_ref[SUB + 1 : SUB + 1 + rows])
        if flow_y[f] is not None:
            flows_ref[SUB : SUB + rows] = flow_y[f]
            for distance, weight in stencil:
                total = total - weight * (
                    flows_ref[SUB + distance : SUB + distance + rows]
                    - flows_ref[SUB - distance : SUB - distance + rows]
                )
        total = total - 6.0 * viscosity * cells[f]
        result.append(cells[f] + time_step * total)
    return result


def sheared(lead, trail, inner):
    first = jnp.where(inner, 1.0 - frac_weight, frac_weight)
    jump = jnp.where(inner, shear_speed, -shear_speed)
    ghosts = [first * a + (1.0 - first) * b for a, b in zip(lead, trail)]
    ghosts[2] = ghosts[2] + jump * ghosts[0]
    return ghosts


def split_pairs(pairs):
    return [pairs[f // 2] if f % 2 == 0 else move(pairs[f // 2], -RIGHT) for f in range(FIELDS)]


def fill_window(window_ref, before_ref, own_ref, after_ref):
    rows = own_ref.shape[1]
    for part, ref in enumerate((before_ref, own_ref, after_ref)):
        window_ref[:, SUB + part * rows : SUB + (part + 1) * rows] = ref[...]


def neighbours(first_ref, second_ref, even):
    return jnp.where(even, second_ref[...], first_ref[...]), jnp.where(even, first_ref[...], second_ref[...])


def axis_place(axis):
    place = lax.axis_index(axis)
    return lax.rem(place, 2), place == 0, place == lax.axis_size(axis) - 1


def edges_kernel(density, momentum, magnetic, tracer, state, near, far, pairs):
    layers, rows, cols = density.shape
    slot = cols // layers
    odd, _, last = axis_place("rad")
    lane = lanes_of((rows, cols))
    width = 2 * REACH
    near_parts, far_parts = [jnp.zeros((rows, cols), jnp.float32)] * 2, [jnp.zeros((rows, cols), jnp.float32)] * 2
    pair_parts = [jnp.zeros((rows, cols), jnp.float32)] * 4
    shift_pair = jnp.where(last, REACH, width)
    for f in range(FIELDS):
        for z in range(layers):
            plane = density[z] if f == 0 else tracer[z] if f == 7 else momentum[f - 1, z] if f < 4 else magnetic[f - 4, z]
            state[f, z] = plane
            start = z * slot + (f % 4) * PACK
            inside = (lane >= start) & (lane < start + PACK)
            left, right = move(plane, start), move(plane, start + width)
            near_parts[f // 4] = jnp.where(inside, jnp.where(odd == 1, right, left), near_parts[f // 4])
            far_parts[f // 4] = jnp.where(inside, jnp.where(odd == 1, left, right), far_parts[f // 4])
            start = z * slot + (f % 2) * RIGHT
            begin = start + jnp.where(last, 0, width)
            inside = (lane >= begin) & (lane < begin + REACH)
            pair_parts[f // 2] = jnp.where(inside, move(plane, start + shift_pair), pair_parts[f // 2])
    for part in range(2):
        near[part], far[part] = near_parts[part], far_parts[part]
    for part in range(4):
        pairs[part] = pair_parts[part]


def join_kernel(pairs, received, joined):
    _, _, last = axis_place("rad")
    slot = 2 * RIGHT
    lane = lax.rem(lanes_of(pairs.shape[1:]), slot)
    offset = jnp.where(last, REACH, 0)
    for part in range(4):
        total = pairs[part]
        for f in (2 * part, 2 * part + 1):
            begin = (f % 2) * RIGHT + offset
            inside = (lane >= begin) & (lane < begin + 2 * REACH)
            total = jnp.where(inside, move(received[f // 4], begin - (f % 4) * PACK), total)
        joined[part] = total


def bulk_kernel(state, near, far, halo, first, second):
    odd, _, _ = axis_place("rad")
    odd_az, _, _ = axis_place("az")
    _, layers, rows, cols = state.shape
    slot = cols // layers
    lane = lax.rem(lanes_of((rows, cols)), slot)
    for f in range(FIELDS):
        a, b = far[f // 4], near[f // 4]
        left, right = jnp.where(odd == 1, a, b), jnp.where(odd == 1, b, a)
        left, right = move(left, -(f % 4) * PACK), move(right, RIGHT + REACH - (f % 4) * PACK)
        halo[f] = jnp.where(
            lane < 2 * REACH,
            left,
            jnp.where((lane >= RIGHT + REACH) & (lane < RIGHT + 3 * REACH), right, 0.0),
        )
    tail = pl.multiple_of((1 - odd_az) * (rows - SUB), SUB)
    head = pl.multiple_of(odd_az * (rows - SUB), SUB)
    planes = FIELDS * layers
    for out, start in ((first, tail), (second, head)):
        for f in range(FIELDS):
            for z in range(layers):
                out[f * layers + z] = state[f, z, pl.ds(start, SUB), :]
            out[planes + f] = halo[f, pl.ds(start, SUB), :]


def far_kernel(offsets, own, first, second, packed, window, flows_ref, cells_ref, *, turn, wrap):
    odd_az, _, _ = axis_place("az")
    _, _, last = axis_place("rad")
    tiles, rows, cols = own.shape
    layers = cols // (2 * RIGHT)
    total_rows = rows * lax.axis_size("az")
    before, after = neighbours(first, second, odd_az == 0)
    fill_window(window, before, own, after)
    shift, turned = offsets[0], offsets[1] - total_rows // 2
    height = rows + SUB
    base = SUB + rows
    begin = jnp.where(last, base - REACH - 1 - turned + wrap * rows, base - REACH + turned - wrap * rows)
    edge = jnp.where(
        last, base - REACH - 1 - turned + turn * rows + shift, base - REACH + turned - turn * rows - shift - 1
    )
    cells = split_pairs([window[t, pl.ds(begin, height), :] for t in range(tiles)])
    lead = split_pairs([window[t, pl.ds(edge, height), :] for t in range(tiles)])
    trail = split_pairs([window[t, pl.ds(edge + 1, height), :] for t in range(tiles)])
    lane = lax.rem(lanes_of((height, cols)), 2 * RIGHT)
    ghost_start = jnp.where(last, 0, 2 * REACH)
    ghost_lane = (lane >= ghost_start) & (lane < ghost_start + REACH)
    ghosts = sheared(lead, trail, last)
    cells = [jnp.where(ghost_lane, g, c) for g, c in zip(ghosts, cells)]
    section = strip_section(cells, flows_ref, cells_ref, layers)
    lead, trail = [], []
    for f in range(FIELDS):
        cells_ref[SUB : SUB + height] = section[f]
        lead.append(cells_ref[SUB + REACH : SUB + REACH + rows])
        trail.append(cells_ref[SUB + REACH + 1 : SUB + REACH + 1 + rows])
    ghosts = sheared(lead, trail, jnp.logical_not(last))
    lane = lax.rem(lanes_of((rows, cols)), 2 * RIGHT)
    for part in range(2):
        total = jnp.zeros((rows, cols), jnp.float32)
        for i in range(4):
            inside = (lane >= i * PACK) & (lane < (i + 1) * PACK)
            total = jnp.where(inside, move(ghosts[4 * part + i], i * PACK - REACH), total)
        packed[part] = total


def ends_to_plane(strip, z, layers):
    return move(strip, -(z * (strip.shape[-1] // layers) + 2 * REACH))


def ends_strip(left, right, lane):
    return jnp.where(lane < 2 * REACH, left, right)


def section_tiles(cells_ref, halo_ref, flow_y, flow_z, partial, layers, tiles, first_row, emit):
    cols = cells_ref.shape[-1]
    lane = lanes_of((SUB, cols))
    weights = layer_weights(layers)
    all_tiles = cells_ref.shape[2] // SUB
    for z in range(layers):
        for t in range(all_tiles):
            span = pl.ds(t * SUB, SUB)
            cells = [cells_ref[f, z, span, :] for f in range(FIELDS)]
            velocity, pressure = primitives(cells)
            flows = flux(cells, velocity, pressure, 1)
            for f in range(FIELDS):
                if flows[f] is not None:
                    flow_y[f, z, span, :] = flows[f]
            if t not in tiles:
                continue
            flows = flux(cells, velocity, pressure, 2)
            for f in range(FIELDS):
                if flows[f] is not None:
                    flow_z[f, z, span, :] = flows[f]
            flows = flux(cells, velocity, pressure, 0)
            halo = [ends_to_plane(halo_ref[f, span, :], z, layers) for f in range(FIELDS)]
            velocity, pressure = primitives(halo)
            halo_flows = flux(halo, velocity, pressure, 0)
            for f in range(FIELDS):
                partial[f, z, span, :] = along_lanes(cells[f], flows[f], lane, halo[f], halo_flows[f])
    for z in range(layers):
        for t in tiles:
            start = t * SUB
            for f in range(FIELDS):
                def near(ref, layer, shift, f=f, start=start):
                    return ref[f, layer, pl.ds(start + shift, SUB), :]

                cells = near(cells_ref, z, 0)
                total = partial[f, z, pl.ds(start, SUB), :]
                around = near(cells_ref, z, 1) + near(cells_ref, z, -1)
                around = around + near(cells_ref, (z + 1) % layers, 0) + near(cells_ref, (z - 1) % layers, 0)
                total = total + viscosity * (around - 6.0 * cells)
                if f != 5:
                    for distance, weight in stencil:
                        total = total - weight * (near(flow_y, z, distance) - near(flow_y, z, -distance))
                if f != 6:
                    for distance, weight in weights.items():
                        total = total - weight * near(flow_z, (z + distance) % layers, 0)
                emit(f, z, t, cells, cells + time_step * total)


def first_kernel(
    offsets, state, own, first, second, halo, first_bulk, second_bulk, section, strips,
    cells_ref, window, halo_ref, flow_y, flow_z, partial, flows_ref, strip_ref, *, wrap,
):
    odd_az, _, _ = axis_place("az")
    _, begins, last = axis_place("rad")
    _, layers, rows, cols = state.shape
    slot = cols // layers
    planes = FIELDS * layers
    height = rows + 2 * SUB
    even = odd_az == 0
    for f in range(FIELDS):
        for z in range(layers):
            a, b = first_bulk[f * layers + z], second_bulk[f * layers + z]
            cells_ref[f, z, SUB : 2 * SUB, :] = jnp.where(even, b, a)
            cells_ref[f, z, 2 * SUB : 2 * SUB + rows, :] = state[f, z]
            cells_ref[f, z, 2 * SUB + rows : 3 * SUB + rows, :] = jnp.where(even, a, b)
    before, after = neighbours(first, second, even)
    fill_window(window, before, own, after)
    begin = jnp.where(last, rows - 1 - offsets[0] + wrap * rows, rows + offsets[0] - wrap * rows)
    lead = split_pairs([window[t, pl.ds(begin, height), :] for t in range(own.shape[0])])
    trail = split_pairs([window[t, pl.ds(begin + 1, height), :] for t in range(own.shape[0])])
    ghosts = sheared(lead, trail, begins)
    lane = lax.rem(lanes_of((height, cols)), slot)
    whole = lanes_of((rows, cols))
    strip_cells = []
    for f in range(FIELDS):
        a, b = first_bulk[planes + f], second_bulk[planes + f]
        strip = jnp.concatenate([jnp.where(even, b, a), halo[f], jnp.where(even, a, b)], axis=0)
        own_part = jnp.zeros((rows, cols), jnp.float32)
        for z in range(layers):
            low = z * slot + 2 * REACH
            own_part = jnp.where((whole >= low) & (whole < low + REACH), move(state[f, z], low), own_part)
            low = z * slot + RIGHT
            own_part = jnp.where((whole >= low) & (whole < low + REACH), move(state[f, z], low + REACH), own_part)
        own_part = jnp.concatenate([jnp.zeros((SUB, cols), jnp.float32), own_part, jnp.zeros((SUB, cols), jnp.float32)], axis=0)
        own_lane = ((lane >= 2 * REACH) & (lane < 3 * REACH)) | ((lane >= RIGHT) & (lane < RIGHT + REACH))
        strip_cells.append(jnp.where(own_lane, own_part, strip))
        right = move(strip, 2 * REACH - RIGHT - REACH)
        left = jnp.where(begins, ghosts[f], strip)
        right = jnp.where(last, move(ghosts[f], REACH), right)
        halo_ref[f, SUB : SUB + height, :] = ends_strip(left, right, lane)
    done = strip_section(strip_cells, flows_ref, strip_ref, layers)
    for f in range(FIELDS):
        right = move(done[f], 2 * REACH - RIGHT - REACH)
        strips[f] = ends_strip(done[f], right, lane)[SUB : SUB + rows]

    def emit(f, z, t, cells, value):
        section[f, z, (t - 1) * SUB : t * SUB, :] = value

    tiles = range(1, 1 + height // SUB)
    section_tiles(cells_ref, halo_ref, flow_y, flow_z, partial, layers, tiles, 0, emit)


def second_kernel(state, section, strips, packed, result, halo_ref, flow_y, flow_z, partial):
    _, begins, last = axis_place("rad")
    _, layers, rows, cols = state.shape
    lane = lax.rem(lanes_of((rows, cols)), cols // layers)
    for f in range(FIELDS):
        ghosts = packed[f // 4]
        left = move(ghosts, REACH - (f % 4) * PACK)
        right = move(ghosts, 2 * REACH - (f % 4) * PACK)
        strip = strips[f]
        halo_ref[f, SUB : SUB + rows, :] = ends_strip(
            jnp.where(begins, left, strip), jnp.where(last, right, strip), lane
        )

    def emit(f, z, t, cells, value):
        rows_of = slice((t - 1) * SUB, t * SUB)
        result[f, z, rows_of, :] = 0.5 * state[f, z, rows_of, :] + 0.5 * value

    tiles = range(1, 1 + rows // SUB)
    section_tiles(section, halo_ref, flow_y, flow_z, partial, layers, tiles, 0, emit)


VMEM = pl.BlockSpec(memory_space=pltpu.VMEM)
SMEM = pl.BlockSpec(memory_space=pltpu.SMEM)


def call(kernel, name, outs, *args, scratch=(), flops=0, smem=0):
    many = isinstance(outs, list)
    return pl.pallas_call(
        kernel,
        name=name,
        out_shape=outs,
        in_specs=[SMEM] * smem + [VMEM] * (len(args) - smem),
        out_specs=[VMEM] * len(outs) if many else VMEM,
        scratch_shapes=[pltpu.VMEM(shape, jnp.float32) for shape in scratch],
        compiler_params=pltpu.CompilerParams(vmem_limit_bytes=24 * 2**20),
        cost_estimate=pl.CostEstimate(flops=flops, bytes_accessed=2**18, transcendentals=0),
    )(*args)


def routes(az_count, rad_count, wrap, turn):
    def listed(target):
        pairs = []
        for a in range(az_count):
            for r in range(rad_count):
                to_a, to_r = target(a, r)
                pairs.append((a * rad_count + r, (to_a % az_count) * rad_count + to_r))
        return pairs

    end = rad_count - 1

    def near(a, r):
        if r == 0:
            return a + wrap, end
        if r == end:
            return a - wrap, 0
        return a, r + 1 if r % 2 else r - 1

    def half_turn(a, r):
        extra = -turn if r == 0 else turn if r == end else 0
        return a + az_count // 2 + extra, r

    return (
        listed(near),
        listed(lambda a, r: (a, r ^ 1)),
        listed(lambda a, r: (a ^ 1, r)),
        listed(lambda a, r: (((a + 1) ^ 1) - 1, r)),
        listed(half_turn),
    )


def exchange_and_step(wrap, turned_wrap, offsets, state, near, far, pairs):
    _, layers, rows, cols = state.shape
    turn = turned_wrap - wrap
    near_route, far_route, first_route, second_route, turn_route = routes(
        lax.axis_size("az"), lax.axis_size("rad"), wrap, turn
    )
    axes = ("az", "rad")
    planes = FIELDS * layers
    near_in = lax.ppermute(near, axes, near_route)
    far_in = lax.ppermute(far, axes, far_route)
    own = call(join_kernel, "join", struct(4, rows, cols), pairs, near_in)
    first = lax.ppermute(own, axes, first_route)
    second = lax.ppermute(own, axes, second_route)
    bulk = struct(planes + FIELDS, SUB, cols)
    halo, to_first, to_second = call(
        bulk_kernel, "bulk", [struct(FIELDS, rows, cols), bulk, bulk], state, near_in, far_in
    )
    first_bulk = lax.ppermute(to_first, axes, first_route)
    second_bulk = lax.ppermute(to_second, axes, second_route)
    window = (4, 3 * rows + 2 * SUB, cols)
    packed = call(
        functools.partial(far_kernel, turn=turn, wrap=turned_wrap),
        "far",
        struct(2, rows, cols),
        offsets,
        own,
        first,
        second,
        scratch=[window] + [(rows + 3 * SUB, cols)] * 2,
        smem=1,
    )
    packed = lax.ppermute(packed, axes, turn_route)
    height = rows + 2 * SUB
    padded = (FIELDS, layers, height + 2 * SUB, cols)
    section, strips = call(
        functools.partial(first_kernel, wrap=wrap),
        "first_section",
        [struct(FIELDS, layers, height, cols), struct(FIELDS, rows, cols)],
        offsets,
        state,
        own,
        first,
        second,
        halo,
        first_bulk,
        second_bulk,
        scratch=[padded, window, (FIELDS, height + 2 * SUB, cols), padded, padded, padded]
        + [(height + 2 * SUB, cols)] * 2,
        smem=1,
        flops=2**23,
    )
    return call(
        second_kernel,
        "second_section",
        struct(FIELDS, layers, rows, cols),
        state,
        section,
        strips,
        packed,
        scratch=[(FIELDS, height, cols)] + [(FIELDS, layers, height, cols)] * 3,
        flops=2**22,
    )


def shards(density, momentum, magnetic, tracer, offsets):
    layers, rows, cols = density.shape
    total_rows = rows * lax.axis_size("az")
    state, near, far, pairs = call(
        edges_kernel,
        "edges",
        [struct(FIELDS, layers, rows, cols), struct(2, rows, cols), struct(2, rows, cols), struct(4, rows, cols)],
        density,
        momentum,
        magnetic,
        tracer,
    )
    crosses = (offsets > jnp.array([rows - 4, rows - 4 + total_rows // 2])).astype(jnp.int32)
    branches = [
        functools.partial(exchange_and_step, wrap, turned_wrap) for wrap in range(2) for turned_wrap in range(2)
    ]
    return lax.switch(2 * crosses[0] + crosses[1], branches, offsets, state, near, far, pairs)


def solution(mesh):
    placed = (
        P(None, "az", "rad"),
        P(None, None, "az", "rad"),
        P(None, None, "az", "rad"),
        P(None, "az", "rad"),
        P(),
    )
    return jax.shard_map(
        shards, mesh=mesh, in_specs=placed, out_specs=P(None, None, "az", "rad"), check_vma=False
    )
```

```python
import functools

import jax
import jax.numpy as jnp
from jax import lax
from jax.experimental import pallas as pl
from jax.experimental.pallas import tpu as pltpu
from jax.sharding import PartitionSpec as P

time_step = 0.025
viscosity = 0.5
sound_squared = 1.0
shear_speed = 1.0
frac_weight = 0.375
stencil = ((1, 45.0 / 60.0), (2, -9.0 / 60.0), (3, 1.0 / 60.0))
REACH = 3
FIELDS = 8
SUB = 8
RIGHT = 16
PACK = 8


def struct(*shape):
    return jax.ShapeDtypeStruct(shape, jnp.float32)


def lanes_of(shape):
    return lax.broadcasted_iota(jnp.int32, shape, len(shape) - 1)


def move(values, by):
    count = values.shape[-1]
    if isinstance(by, int):
        by = by % count
        return values if by == 0 else pltpu.roll(values, by, values.ndim - 1)
    return pltpu.roll(values, lax.rem(by + count, count), values.ndim - 1)


def primitives(cells):
    inverse = 1.0 / cells[0]
    velocity = [cells[1 + i] * inverse for i in range(3)]
    squares = cells[4] * cells[4] + cells[5] * cells[5] + cells[6] * cells[6]
    return velocity, sound_squared * cells[0] + 0.5 * squares


def flux(cells, velocity, pressure, direction):
    speed, normal = velocity[direction], cells[4 + direction]
    result = [cells[1 + direction]]
    for i in range(3):
        term = cells[1 + i] * speed - cells[4 + i] * normal
        result.append(term + pressure if i == direction else term)
    for i in range(3):
        result.append(None if i == direction else speed * cells[4 + i] - normal * velocity[i])
    result.append(cells[7] * speed)
    return result


def along_lanes(values, flows, lane, halo_values=None, halo_flows=None):
    count = values.shape[-1]

    def ends(array, halo, width):
        if halo is None:
            return array, array
        return jnp.where(lane < width, halo, array), jnp.where(lane >= count - width, halo, array)

    above, below = ends(values, halo_values, 1)
    up, down = viscosity * above, viscosity * below
    if flows is None:
        return move(up, -1) + move(down, 1)
    total = None
    for distance, weight in stencil:
        above, below = ends(flows, halo_flows, distance)
        plus, minus = -weight * above, weight * below
        if distance == 1:
            plus, minus = plus + up, minus + down
        pair = move(plus, -distance) + move(minus, distance)
        total = pair if total is None else total + pair
    return total


def layer_weights(layers):
    folded = {}
    for distance, weight in stencil:
        for signed, share in ((distance, weight), (-distance, -weight)):
            folded[signed % layers] = folded.get(signed % layers, 0.0) + share
    return {distance: weight for distance, weight in folded.items() if weight != 0.0 and distance != 0}


def strip_section(cells, flows_ref, cells_ref, layers):
    rows, count = cells[0].shape
    slot = count // layers
    velocity, pressure = primitives(cells)
    flow_x, flow_y, flow_z = (flux(cells, velocity, pressure, d) for d in range(3))
    weights = layer_weights(layers)
    result = []
    for f in range(FIELDS):
        cells_ref[f, SUB : SUB + rows] = cells[f]
        if flow_y[f] is not None:
            flows_ref[f, SUB : SUB + rows] = flow_y[f]
    for f in range(FIELDS):
        total = along_lanes(cells[f], flow_x[f], None)
        total = total + viscosity * (move(cells[f], slot) + move(cells[f], -slot))
        if flow_z[f] is not None:
            for distance, weight in weights.items():
                total = total - weight * move(flow_z[f], -distance * slot)
        total = total + viscosity * (cells_ref[f, SUB - 1 : SUB - 1 + rows] + cells_ref[f, SUB + 1 : SUB + 1 + rows])
        if flow_y[f] is not None:
            for distance, weight in stencil:
                total = total - weight * (
                    flows_ref[f, SUB + distance : SUB + distance + rows]
                    - flows_ref[f, SUB - distance : SUB - distance + rows]
                )
        total = total - 6.0 * viscosity * cells[f]
        result.append(cells[f] + time_step * total)
    return result


def sheared(lead, trail, inner):
    first = jnp.where(inner, 1.0 - frac_weight, frac_weight)
    jump = jnp.where(inner, shear_speed, -shear_speed)
    ghosts = [first * a + (1.0 - first) * b for a, b in zip(lead, trail)]
    ghosts[2] = ghosts[2] + jump * ghosts[0]
    return ghosts


def split_pairs(pairs):
    return [pairs[f // 2] if f % 2 == 0 else move(pairs[f // 2], -RIGHT) for f in range(FIELDS)]


def fill_window(window_ref, own_ref, first_ref, second_ref, even):
    tiles, rows, _ = own_ref.shape
    parts = rows // SUB
    for t in range(tiles):
        window_ref[t, SUB + rows : SUB + 2 * rows] = own_ref[t]
        for i in range(parts):
            before, after = neighbours(first_ref[t * parts + i], second_ref[t * parts + i], even)
            window_ref[t, SUB + i * SUB : SUB + (i + 1) * SUB] = before
            window_ref[t, SUB + 2 * rows + i * SUB : SUB + 2 * rows + (i + 1) * SUB] = after


def neighbours(first, second, even):
    return jnp.where(even, second, first), jnp.where(even, first, second)


def axis_place(axis):
    place = lax.axis_index(axis)
    return lax.rem(place, 2), place == 0, place == lax.axis_size(axis) - 1


def rows_for(rows):
    odd, _, _ = axis_place("az")
    return pl.multiple_of((1 - odd) * (rows - SUB), SUB), pl.multiple_of(odd * (rows - SUB), SUB)


def edges_kernel(density, momentum, magnetic, tracer, offsets, state, near, far, pairs, index, shifts, *rest):
    *bulks, held, sems = rest
    layers, rows, cols = density.shape
    slot = cols // layers
    parts = (
        (density, state.at[0]),
        (momentum, state.at[1:4]),
        (magnetic, state.at[4:7]),
        (tracer, state.at[7]),
        (offsets, held),
    )
    copies = [pltpu.make_async_copy(source, target, sems.at[i]) for i, (source, target) in enumerate(parts)]
    for copy in copies:
        copy.start()
    odd, _, last = axis_place("rad")
    lane = lanes_of((rows, cols))
    width = 2 * REACH
    near_parts, far_parts = [jnp.zeros((rows, cols), jnp.float32)] * 2, [jnp.zeros((rows, cols), jnp.float32)] * 2
    pair_parts = [jnp.zeros((rows, cols), jnp.float32)] * 4
    shift_pair = jnp.where(last, REACH, width)
    for f in range(FIELDS):
        if f in (0, 1, 4, 7):
            copies[(0, 1, 4, 7).index(f)].wait()
        for z in range(layers):
            plane = state[f, z]
            start = z * slot + (f % 4) * PACK
            inside = (lane >= start) & (lane < start + PACK)
            left, right = move(plane, start), move(plane, start + width)
            near_parts[f // 4] = jnp.where(inside, jnp.where(odd == 1, right, left), near_parts[f // 4])
            far_parts[f // 4] = jnp.where(inside, jnp.where(odd == 1, left, right), far_parts[f // 4])
            start = z * slot + (f % 2) * RIGHT
            begin = start + jnp.where(last, 0, width)
            inside = (lane >= begin) & (lane < begin + REACH)
            pair_parts[f // 2] = jnp.where(inside, move(plane, start + shift_pair), pair_parts[f // 2])
    for part in range(2):
        near[part], far[part] = near_parts[part], far_parts[part]
    for part in range(2, far.shape[0]):
        far[part] = jnp.zeros((rows, cols), jnp.float32)
    for part in range(2, near.shape[0]):
        near[part] = jnp.zeros((rows, cols), jnp.float32)
    for part in range(4):
        pairs[part] = pair_parts[part]
    odd_az, _, _ = axis_place("az")
    for f in range(FIELDS):
        for z in range(layers):
            head, tail = state[f, z, :width, :], state[f, z, rows - width :, :]
            place = slice((f * layers + z) * width, (f * layers + z + 1) * width)
            bulks[0][place, :] = jnp.where(odd_az == 1, head, tail)
            bulks[1][place, :] = jnp.where(odd_az == 1, tail, head)
    copies[4].wait()
    half = rows * lax.axis_size("az") // 2
    for i in range(2):
        shifts[i : i + 1, :] = jnp.full((1, cols), held[i])
    index[...] = jnp.full((1,), jnp.where(held[0] > rows - 4, 2, 0) + jnp.where(held[1] > rows - 4 + half, 1, 0))


def join_kernel(pairs, near, far, own, halo, first, second):
    odd, _, last = axis_place("rad")
    tiles, rows, cols = pairs.shape
    slot = 2 * RIGHT
    lane = lax.rem(lanes_of((rows, cols)), slot)
    offset = jnp.where(last, REACH, 0)
    parts = rows // SUB
    starts = rows_for(rows)
    for part in range(tiles):
        total = pairs[part]
        for f in (2 * part, 2 * part + 1):
            begin = (f % 2) * RIGHT + offset
            inside = (lane >= begin) & (lane < begin + 2 * REACH)
            total = jnp.where(inside, move(near[f // 4], begin - (f % 4) * PACK), total)
        own[part] = total
        for i in range(parts):
            first[part * parts + i] = second[part * parts + i] = total[i * SUB : (i + 1) * SUB]
    for f in range(FIELDS):
        a, b = far[f // 4], near[f // 4]
        left, right = jnp.where(odd == 1, a, b), jnp.where(odd == 1, b, a)
        left, right = move(left, -(f % 4) * PACK), move(right, RIGHT + REACH - (f % 4) * PACK)
        halo[f] = jnp.where(
            lane < 2 * REACH,
            left,
            jnp.where((lane >= RIGHT + REACH) & (lane < RIGHT + 3 * REACH), right, 0.0),
        )
        for out, start in zip((first, second), starts):
            out[tiles * parts + f] = halo[f, pl.ds(start, SUB), :]


def far_kernel(offsets, own, first, second, packed, window, flows_ref, cells_ref, *, turn, wrap):
    odd_az, _, _ = axis_place("az")
    _, _, last = axis_place("rad")
    tiles, rows, cols = own.shape
    layers = cols // (2 * RIGHT)
    total_rows = rows * lax.axis_size("az")
    fill_window(window, own, first, second, odd_az == 0)
    shift, turned = offsets[0, 0], offsets[1, 0] - total_rows // 2
    height = rows + SUB
    base = SUB + rows
    begin = jnp.where(last, base - REACH - 1 - turned + wrap * rows, base - REACH + turned - wrap * rows)
    edge = jnp.where(
        last, base - REACH - 1 - turned + turn * rows + shift, base - REACH + turned - turn * rows - shift - 1
    )
    cells = split_pairs([window[t, pl.ds(begin, height), :] for t in range(tiles)])
    lead = split_pairs([window[t, pl.ds(edge, height), :] for t in range(tiles)])
    trail = split_pairs([window[t, pl.ds(edge + 1, height), :] for t in range(tiles)])
    lane = lax.rem(lanes_of((height, cols)), 2 * RIGHT)
    ghost_start = jnp.where(last, 0, 2 * REACH)
    ghost_lane = (lane >= ghost_start) & (lane < ghost_start + REACH)
    ghosts = sheared(lead, trail, last)
    cells = [jnp.where(ghost_lane, g, c) for g, c in zip(ghosts, cells)]
    section = strip_section(cells, flows_ref, cells_ref, layers)
    lead, trail = [], []
    for f in range(FIELDS):
        flows_ref[f, SUB : SUB + height] = section[f]
        lead.append(flows_ref[f, SUB + REACH : SUB + REACH + rows])
        trail.append(flows_ref[f, SUB + REACH + 1 : SUB + REACH + 1 + rows])
    ghosts = sheared(lead, trail, jnp.logical_not(last))
    lane = lax.rem(lanes_of((rows, cols)), 2 * RIGHT)
    for part in range(2):
        total = jnp.zeros((rows, cols), jnp.float32)
        for i in range(4):
            inside = (lane >= i * PACK) & (lane < (i + 1) * PACK)
            total = jnp.where(inside, move(ghosts[4 * part + i], i * PACK - REACH), total)
        packed[part] = total


def section_tiles(cells_ref, flow_y, flow_z, partial, tiles, emit):
    _, layers, rows, cols = cells_ref.shape
    lane = lanes_of((SUB, cols))
    weights = layer_weights(layers)
    for z in range(layers):
        for t in range(rows // SUB):
            span = pl.ds(t * SUB, SUB)
            cells = [cells_ref[f, z, span, :] for f in range(FIELDS)]
            velocity, pressure = primitives(cells)
            flows = flux(cells, velocity, pressure, 1)
            for f in range(FIELDS):
                if flows[f] is not None:
                    flow_y[f, z, span, :] = flows[f]
            if t not in tiles:
                continue
            flows = flux(cells, velocity, pressure, 2)
            for f in range(FIELDS):
                if flows[f] is not None:
                    flow_z[f, z, span, :] = flows[f]
            flows = flux(cells, velocity, pressure, 0)
            for f in range(FIELDS):
                partial[f, z, span, :] = along_lanes(cells[f], flows[f], lane, 0.0, 0.0)
    for z in range(layers):
        for t in tiles:
            start = t * SUB
            for f in range(FIELDS):

                def near(ref, layer, shift, f=f, start=start):
                    return ref[f, layer, pl.ds(start + shift, SUB), :]

                cells = near(cells_ref, z, 0)
                total = partial[f, z, pl.ds(start, SUB), :]
                around = near(cells_ref, z, 1) + near(cells_ref, z, -1)
                around = around + near(cells_ref, (z + 1) % layers, 0) + near(cells_ref, (z - 1) % layers, 0)
                total = total + viscosity * (around - 6.0 * cells)
                if f != 5:
                    for distance, weight in stencil:
                        total = total - weight * (near(flow_y, z, distance) - near(flow_y, z, -distance))
                if f != 6:
                    for distance, weight in weights.items():
                        total = total - weight * near(flow_z, (z + distance) % layers, 0)
                emit(f, z, t, cells + time_step * total)


def end_terms(halo, layers):
    lane = lax.rem(lanes_of(halo[0].shape), halo[0].shape[-1] // layers)
    low, high = (lane >= REACH) & (lane < 2 * REACH), (lane >= 2 * REACH) & (lane < 3 * REACH)
    velocity, pressure = primitives(halo)
    flows = flux(halo, velocity, pressure, 0)
    result = []
    for f in range(FIELDS):
        up, down = move(halo[f], 1), move(halo[f], -1)
        from_low = jnp.where(lane < 2 * REACH + 1, viscosity * up, 0.0)
        from_high = jnp.where(lane >= 2 * REACH - 1, viscosity * down, 0.0)
        if flows[f] is not None:
            for distance, weight in stencil:
                from_low = from_low + jnp.where(lane < 2 * REACH + distance, weight * move(flows[f], distance), 0.0)
                from_high = from_high - jnp.where(lane >= 2 * REACH - distance, weight * move(flows[f], -distance), 0.0)
        result.append(jnp.where(high, from_low, jnp.where(low, from_high, 0.0)))
    return result


def to_plane(strip, z, layers):
    return move(strip, -(z * (strip.shape[-1] // layers) + 2 * REACH))


def ends_strip(left, right, lane):
    return jnp.where(lane < 2 * REACH, left, right)


def first_kernel(state, first, second, section, cells_ref, flow_y, flow_z, partial):
    odd_az, _, _ = axis_place("az")
    _, layers, rows, _ = state.shape
    even = odd_az == 0
    width = 2 * REACH
    for f in range(FIELDS):
        for z in range(layers):
            place = slice((f * layers + z) * width, (f * layers + z + 1) * width)
            before, after = neighbours(first[place, :], second[place, :], even)
            cells_ref[f, z, 2 * SUB - width : 2 * SUB, :] = before
            cells_ref[f, z, 2 * SUB : 2 * SUB + rows, :] = state[f, z]
            cells_ref[f, z, 2 * SUB + rows : 2 * SUB + rows + width, :] = after

    def emit(f, z, t, value):
        section[f, z, (t - 1) * SUB : t * SUB, :] = value

    section_tiles(cells_ref, flow_y, flow_z, partial, range(1, 3 + rows // SUB), emit)


def ends_kernel(shifts, state, own, first, second, halo, partial, section, strips, window, flows_ref, strip_ref, *, wrap):
    odd_az, _, _ = axis_place("az")
    _, begins, last = axis_place("rad")
    _, layers, rows, cols = state.shape
    slot = cols // layers
    height = rows + 2 * SUB
    even = odd_az == 0
    fill_window(window, own, first, second, even)
    shift = shifts[0, 0]
    begin = jnp.where(last, rows - 1 - shift + wrap * rows, rows + shift - wrap * rows)
    lead = split_pairs([window[t, pl.ds(begin, height), :] for t in range(own.shape[0])])
    trail = split_pairs([window[t, pl.ds(begin + 1, height), :] for t in range(own.shape[0])])
    ghosts = sheared(lead, trail, begins)
    lane = lax.rem(lanes_of((height, cols)), slot)
    whole = lanes_of((rows, cols))
    own_lane = ((lane >= 2 * REACH) & (lane < 3 * REACH)) | ((lane >= RIGHT) & (lane < RIGHT + REACH))
    blank = jnp.zeros((SUB, cols), jnp.float32)
    strip_cells, beyond = [], []
    for f in range(FIELDS):
        corner = first.shape[0] - FIELDS + f
        before, after = neighbours(first[corner], second[corner], even)
        strip = jnp.concatenate([before, halo[f], after], axis=0)
        own_part = jnp.zeros((rows, cols), jnp.float32)
        for z in range(layers):
            low = z * slot + 2 * REACH
            own_part = jnp.where((whole >= low) & (whole < low + REACH), move(state[f, z], low), own_part)
            low = z * slot + RIGHT
            own_part = jnp.where((whole >= low) & (whole < low + REACH), move(state[f, z], low + REACH), own_part)
        own_part = jnp.concatenate([blank, own_part, blank], axis=0)
        strip_cells.append(jnp.where(own_lane, own_part, strip))
        right = move(strip, 2 * REACH - RIGHT - REACH)
        left = jnp.where(begins, ghosts[f], strip)
        right = jnp.where(last, move(ghosts[f], REACH), right)
        beyond.append(ends_strip(left, right, lane))
    terms = end_terms(beyond, layers)
    column = lanes_of((height, cols))
    ends = (column < REACH) | (column >= cols - REACH)
    for f in range(FIELDS):
        for z in range(layers):
            added = jnp.where(ends, time_step * to_plane(terms[f], z, layers), 0.0)
            section[f, z] = partial[f, z] + added
    done = strip_section(strip_cells, flows_ref, strip_ref, layers)
    for f in range(FIELDS):
        right = move(done[f], 2 * REACH - RIGHT - REACH)
        strips[f] = ends_strip(done[f], right, lane)[SUB : SUB + rows]


def second_kernel(state, section, result, flow_y, flow_z, partial):
    _, _, rows, _ = state.shape

    def emit(f, z, t, value):
        rows_of = slice((t - 1) * SUB, t * SUB)
        result[f, z, rows_of, :] = 0.5 * state[f, z, rows_of, :] + 0.5 * value

    section_tiles(section, flow_y, flow_z, partial, range(1, 1 + rows // SUB), emit)


def last_kernel(partial, strips, packed, result):
    _, begins, last = axis_place("rad")
    _, layers, rows, cols = partial.shape
    lane = lax.rem(lanes_of((rows, cols)), cols // layers)
    halo = []
    for f in range(FIELDS):
        ghosts = packed[f // 4]
        left = jnp.where(begins, move(ghosts, REACH - (f % 4) * PACK), strips[f])
        right = jnp.where(last, move(ghosts, 2 * REACH - (f % 4) * PACK), strips[f])
        halo.append(ends_strip(left, right, lane))
    terms = end_terms(halo, layers)
    column = lanes_of((rows, cols))
    ends = (column < REACH) | (column >= cols - REACH)
    for f in range(FIELDS):
        for z in range(layers):
            added = jnp.where(ends, 0.5 * time_step * to_plane(terms[f], z, layers), 0.0)
            result[f, z] = partial[f, z] + added


VMEM = pl.BlockSpec(memory_space=pltpu.VMEM)
SMEM = pl.BlockSpec(memory_space=pltpu.SMEM)
HBM = pl.BlockSpec(memory_space=pltpu.HBM)


BIG = 63 * 2**20


def call(kernel, name, outs, *args, scratch=(), flops=0, smem=0, hbm=0, sems=0, out_spec=VMEM, limit=24 * 2**20, cost=2**18):
    many = isinstance(outs, list)
    scratch_shapes = [pltpu.VMEM(shape, jnp.float32) for shape in scratch]
    if sems:
        scratch_shapes.append(pltpu.SemaphoreType.DMA((sems,)))
    return pl.pallas_call(
        kernel,
        name=name,
        out_shape=outs,
        in_specs=[SMEM] * smem + [HBM] * hbm + [VMEM] * (len(args) - smem - hbm),
        out_specs=[out_spec] * len(outs) if many else out_spec,
        scratch_shapes=scratch_shapes,
        compiler_params=pltpu.CompilerParams(vmem_limit_bytes=limit),
        cost_estimate=pl.CostEstimate(flops=flops, bytes_accessed=cost, transcendentals=0),
    )(*args)


def routes(az_count, rad_count, wrap, turn):
    def listed(target):
        pairs = []
        for a in range(az_count):
            for r in range(rad_count):
                to_a, to_r = target(a, r)
                pairs.append((a * rad_count + r, (to_a % az_count) * rad_count + to_r))
        return pairs

    end = rad_count - 1

    def near(a, r):
        if r == 0:
            return a + wrap, end
        if r == end:
            return a - wrap, 0
        return a, r + 1 if r % 2 else r - 1

    def half_turn(a, r):
        extra = -turn if r == 0 else turn if r == end else 0
        return a + az_count // 2 + extra, r

    return (
        listed(near),
        listed(lambda a, r: (a, r ^ 1)),
        listed(lambda a, r: (a ^ 1, r)),
        listed(lambda a, r: (((a + 1) ^ 1) - 1, r)),
        listed(half_turn),
    )


def exchange_and_step(wrap, turned_wrap, shifts, state, near, far, pairs, *bulks):
    _, layers, rows, cols = state.shape
    turn = turned_wrap - wrap
    near_route, far_route, first_route, second_route, turn_route = routes(
        lax.axis_size("az"), lax.axis_size("rad"), wrap, turn
    )
    axes = ("az", "rad")
    far_in = lax.ppermute(far, axes, far_route)
    near_in = lax.ppermute(near, axes, near_route)
    bulks = [lax.ppermute(part, axes, (first_route, second_route)[i]) for i, part in enumerate(bulks)]
    parcel = struct(4 * rows // SUB + FIELDS, SUB, cols)
    own, halo, for_first, for_second = call(
        join_kernel,
        "join",
        [struct(4, rows, cols), struct(FIELDS, rows, cols), parcel, parcel],
        pairs,
        near_in,
        far_in,
    )
    first = lax.ppermute(for_first, axes, first_route)
    second = lax.ppermute(for_second, axes, second_route)
    height = rows + 2 * SUB
    padded = (FIELDS, layers, height + 2 * SUB, cols)
    partial = call(
        first_kernel,
        "first_section",
        struct(FIELDS, layers, height, cols),
        state,
        *bulks,
        scratch=[padded] * 4,
    )
    window = (4, 3 * rows + 2 * SUB, cols)
    packed = call(
        functools.partial(far_kernel, turn=turn, wrap=turned_wrap),
        "far",
        struct(2, rows, cols),
        shifts,
        own,
        first,
        second,
        scratch=[window] + [(FIELDS, rows + 3 * SUB, cols)] * 2,
    )
    packed = lax.ppermute(packed, axes, turn_route)
    section, strips = call(
        functools.partial(ends_kernel, wrap=wrap),
        "first_ends",
        [struct(FIELDS, layers, height, cols), struct(FIELDS, rows, cols)],
        shifts,
        state,
        own,
        first,
        second,
        halo,
        partial,
        scratch=[window] + [(FIELDS, height + 2 * SUB, cols)] * 2,
    )
    partial = call(
        second_kernel,
        "second_section",
        struct(FIELDS, layers, rows, cols),
        state,
        section,
        scratch=[(FIELDS, layers, height, cols)] * 3,
    )
    return call(last_kernel, "second_ends", struct(FIELDS, layers, rows, cols), partial, strips, packed)


def shards(density, momentum, magnetic, tracer, offsets):
    layers, rows, cols = density.shape
    state, near, far, pairs, index, shifts, *bulks = pl.pallas_call(
        edges_kernel,
        name="edges",
        out_shape=[
            struct(FIELDS, layers, rows, cols),
            struct(3, rows, cols),
            struct(4, rows, cols),
            struct(4, rows, cols),
            jax.ShapeDtypeStruct((1,), jnp.int32),
            jax.ShapeDtypeStruct((SUB, cols), jnp.int32),
        ]
        + [struct(FIELDS * layers * 2 * REACH, cols)] * 2,
        in_specs=[HBM] * 5,
        out_specs=[VMEM] * 8,
        scratch_shapes=[pltpu.SMEM((2,), jnp.int32), pltpu.SemaphoreType.DMA((5,))],
        compiler_params=pltpu.CompilerParams(vmem_limit_bytes=BIG),
    )(density, momentum, magnetic, tracer, offsets)
    branches = [
        functools.partial(exchange_and_step, wrap, turned_wrap) for wrap in range(2) for turned_wrap in range(2)
    ]
    return lax.switch(index[0], branches, shifts, state, near, far, pairs, *bulks)


def solution(mesh):
    placed = (
        P(None, "az", "rad"),
        P(None, None, "az", "rad"),
        P(None, None, "az", "rad"),
        P(None, "az", "rad"),
        P(),
    )
    return jax.shard_map(
        shards, mesh=mesh, in_specs=placed, out_specs=P(None, None, "az", "rad"), check_vma=False
    )
```

```python
import functools

import jax
import jax.numpy as jnp
from jax import lax
from jax.experimental import pallas as pl
from jax.experimental.pallas import tpu as pltpu
from jax.sharding import PartitionSpec as P

time_step = 0.025
viscosity = 0.5
sound_squared = 1.0
shear_speed = 1.0
frac_weight = 0.375
stencil = ((1, 45.0 / 60.0), (2, -9.0 / 60.0), (3, 1.0 / 60.0))
REACH = 3
FIELDS = 8
SUB = 8
RIGHT = 16
PACK = 8


def struct(*shape):
    return jax.ShapeDtypeStruct(shape, jnp.float32)


def lanes_of(shape):
    return lax.broadcasted_iota(jnp.int32, shape, len(shape) - 1)


def move(values, by):
    count = values.shape[-1]
    if isinstance(by, int):
        by = by % count
        return values if by == 0 else pltpu.roll(values, by, values.ndim - 1)
    return pltpu.roll(values, lax.rem(by + count, count), values.ndim - 1)


def primitives(cells):
    inverse = 1.0 / cells[0]
    velocity = [cells[1 + i] * inverse for i in range(3)]
    squares = cells[4] * cells[4] + cells[5] * cells[5] + cells[6] * cells[6]
    return velocity, sound_squared * cells[0] + 0.5 * squares


def flux(cells, velocity, pressure, direction):
    speed, normal = velocity[direction], cells[4 + direction]
    result = [cells[1 + direction]]
    for i in range(3):
        term = cells[1 + i] * speed - cells[4 + i] * normal
        result.append(term + pressure if i == direction else term)
    for i in range(3):
        result.append(None if i == direction else speed * cells[4 + i] - normal * velocity[i])
    result.append(cells[7] * speed)
    return result


def along_lanes(values, flows, lane, halo_values=None, halo_flows=None):
    count = values.shape[-1]

    def ends(array, halo, width):
        if halo is None:
            return array, array
        return jnp.where(lane < width, halo, array), jnp.where(lane >= count - width, halo, array)

    above, below = ends(values, halo_values, 1)
    up, down = viscosity * above, viscosity * below
    if flows is None:
        return move(up, -1) + move(down, 1)
    total = None
    for distance, weight in stencil:
        above, below = ends(flows, halo_flows, distance)
        plus, minus = -weight * above, weight * below
        if distance == 1:
            plus, minus = plus + up, minus + down
        pair = move(plus, -distance) + move(minus, distance)
        total = pair if total is None else total + pair
    return total


def layer_weights(layers):
    folded = {}
    for distance, weight in stencil:
        for signed, share in ((distance, weight), (-distance, -weight)):
            folded[signed % layers] = folded.get(signed % layers, 0.0) + share
    return {distance: weight for distance, weight in folded.items() if weight != 0.0 and distance != 0}


def strip_section(cells, flows_ref, cells_ref, layers):
    rows, count = cells[0].shape
    slot = count // layers
    velocity, pressure = primitives(cells)
    flow_x, flow_y, flow_z = (flux(cells, velocity, pressure, d) for d in range(3))
    weights = layer_weights(layers)
    result = []
    for f in range(FIELDS):
        cells_ref[f, SUB : SUB + rows] = cells[f]
        if flow_y[f] is not None:
            flows_ref[f, SUB : SUB + rows] = flow_y[f]
    for f in range(FIELDS):
        total = along_lanes(cells[f], flow_x[f], None)
        total = total + viscosity * (move(cells[f], slot) + move(cells[f], -slot))
        if flow_z[f] is not None:
            for distance, weight in weights.items():
                total = total - weight * move(flow_z[f], -distance * slot)
        total = total + viscosity * (cells_ref[f, SUB - 1 : SUB - 1 + rows] + cells_ref[f, SUB + 1 : SUB + 1 + rows])
        if flow_y[f] is not None:
            for distance, weight in stencil:
                total = total - weight * (
                    flows_ref[f, SUB + distance : SUB + distance + rows]
                    - flows_ref[f, SUB - distance : SUB - distance + rows]
                )
        total = total - 6.0 * viscosity * cells[f]
        result.append(cells[f] + time_step * total)
    return result


def sheared(lead, trail, inner):
    first = jnp.where(inner, 1.0 - frac_weight, frac_weight)
    jump = jnp.where(inner, shear_speed, -shear_speed)
    ghosts = [first * a + (1.0 - first) * b for a, b in zip(lead, trail)]
    ghosts[2] = ghosts[2] + jump * ghosts[0]
    return ghosts


def split_pairs(pairs):
    return [pairs[f // 2] if f % 2 == 0 else move(pairs[f // 2], -RIGHT) for f in range(FIELDS)]


def fill_window(window_ref, own_ref, first_ref, second_ref, even):
    tiles, rows, _ = own_ref.shape
    parts = rows // SUB
    for t in range(tiles):
        window_ref[t, SUB + rows : SUB + 2 * rows] = own_ref[t]
        for i in range(parts):
            before, after = neighbours(first_ref[t * parts + i], second_ref[t * parts + i], even)
            window_ref[t, SUB + i * SUB : SUB + (i + 1) * SUB] = before
            window_ref[t, SUB + 2 * rows + i * SUB : SUB + 2 * rows + (i + 1) * SUB] = after


def neighbours(first, second, even):
    return jnp.where(even, second, first), jnp.where(even, first, second)


def axis_place(axis):
    place = lax.axis_index(axis)
    return lax.rem(place, 2), place == 0, place == lax.axis_size(axis) - 1


def rows_for(rows):
    odd, _, _ = axis_place("az")
    return pl.multiple_of((1 - odd) * (rows - SUB), SUB), pl.multiple_of(odd * (rows - SUB), SUB)


def edges_kernel(density, momentum, magnetic, tracer, offsets, state, near, far, pairs, index, shifts, *rest):
    *bulks, held, chosen, sems = rest
    layers, rows, cols = density.shape
    slot = cols // layers
    parts = (
        (density, state.at[0]),
        (momentum, state.at[1:4]),
        (magnetic, state.at[4:7]),
        (tracer, state.at[7]),
        (offsets, held),
    )
    copies = [pltpu.make_async_copy(source, target, sems.at[i]) for i, (source, target) in enumerate(parts)]
    for copy in copies:
        copy.start()
    copies[4].wait()
    half = rows * lax.axis_size("az") // 2
    chosen[0] = jnp.where(held[0] > rows - 4, 2, 0) + jnp.where(held[1] > rows - 4 + half, 1, 0)
    chosen_copy = pltpu.make_async_copy(chosen, index, sems.at[5])
    chosen_copy.start()
    for i in range(2):
        shifts[i : i + 1, :] = jnp.full((1, cols), held[i])
    odd, _, last = axis_place("rad")
    lane = lanes_of((rows, cols))
    width = 2 * REACH
    near_parts, far_parts = [jnp.zeros((rows, cols), jnp.float32)] * 2, [jnp.zeros((rows, cols), jnp.float32)] * 2
    pair_parts = [jnp.zeros((rows, cols), jnp.float32)] * 4
    shift_pair = jnp.where(last, REACH, width)
    for f in range(FIELDS):
        if f in (0, 1, 4, 7):
            copies[(0, 1, 4, 7).index(f)].wait()
        for z in range(layers):
            plane = state[f, z]
            start = z * slot + (f % 4) * PACK
            inside = (lane >= start) & (lane < start + PACK)
            left, right = move(plane, start), move(plane, start + width)
            near_parts[f // 4] = jnp.where(inside, jnp.where(odd == 1, right, left), near_parts[f // 4])
            far_parts[f // 4] = jnp.where(inside, jnp.where(odd == 1, left, right), far_parts[f // 4])
            start = z * slot + (f % 2) * RIGHT
            begin = start + jnp.where(last, 0, width)
            inside = (lane >= begin) & (lane < begin + REACH)
            pair_parts[f // 2] = jnp.where(inside, move(plane, start + shift_pair), pair_parts[f // 2])
    for part in range(2):
        near[part], far[part] = near_parts[part], far_parts[part]
    for part in range(2, far.shape[0]):
        far[part] = jnp.zeros((rows, cols), jnp.float32)
    for part in range(2, near.shape[0]):
        near[part] = jnp.zeros((rows, cols), jnp.float32)
    for part in range(4):
        pairs[part] = pair_parts[part]
    odd_az, _, _ = axis_place("az")
    for f in range(FIELDS):
        for z in range(layers):
            head, tail = state[f, z, :width, :], state[f, z, rows - width :, :]
            place = slice((f * layers + z) * width, (f * layers + z + 1) * width)
            bulks[0][place, :] = jnp.where(odd_az == 1, head, tail)
            bulks[1][place, :] = jnp.where(odd_az == 1, tail, head)
    chosen_copy.wait()


def join_kernel(pairs, near, far, own, halo, first, second):
    odd, _, last = axis_place("rad")
    tiles, rows, cols = pairs.shape
    slot = 2 * RIGHT
    lane = lax.rem(lanes_of((rows, cols)), slot)
    offset = jnp.where(last, REACH, 0)
    parts = rows // SUB
    starts = rows_for(rows)
    for part in range(tiles):
        total = pairs[part]
        for f in (2 * part, 2 * part + 1):
            begin = (f % 2) * RIGHT + offset
            inside = (lane >= begin) & (lane < begin + 2 * REACH)
            total = jnp.where(inside, move(near[f // 4], begin - (f % 4) * PACK), total)
        own[part] = total
        for i in range(parts):
            first[part * parts + i] = second[part * parts + i] = total[i * SUB : (i + 1) * SUB]
    for f in range(FIELDS):
        a, b = far[f // 4], near[f // 4]
        left, right = jnp.where(odd == 1, a, b), jnp.where(odd == 1, b, a)
        left, right = move(left, -(f % 4) * PACK), move(right, RIGHT + REACH - (f % 4) * PACK)
        halo[f] = jnp.where(
            lane < 2 * REACH,
            left,
            jnp.where((lane >= RIGHT + REACH) & (lane < RIGHT + 3 * REACH), right, 0.0),
        )
        for out, start in zip((first, second), starts):
            out[tiles * parts + f] = halo[f, pl.ds(start, SUB), :]


def far_kernel(offsets, own, first, second, _, packed, window, flows_ref, cells_ref, *, turn, wrap):
    odd_az, _, _ = axis_place("az")
    _, _, last = axis_place("rad")
    tiles, rows, cols = own.shape
    layers = cols // (2 * RIGHT)
    total_rows = rows * lax.axis_size("az")
    fill_window(window, own, first, second, odd_az == 0)
    shift, turned = offsets[0, 0], offsets[1, 0] - total_rows // 2
    height = rows + SUB
    base = SUB + rows
    begin = jnp.where(last, base - REACH - 1 - turned + wrap * rows, base - REACH + turned - wrap * rows)
    edge = jnp.where(
        last, base - REACH - 1 - turned + turn * rows + shift, base - REACH + turned - turn * rows - shift - 1
    )
    cells = split_pairs([window[t, pl.ds(begin, height), :] for t in range(tiles)])
    lead = split_pairs([window[t, pl.ds(edge, height), :] for t in range(tiles)])
    trail = split_pairs([window[t, pl.ds(edge + 1, height), :] for t in range(tiles)])
    lane = lax.rem(lanes_of((height, cols)), 2 * RIGHT)
    ghost_start = jnp.where(last, 0, 2 * REACH)
    ghost_lane = (lane >= ghost_start) & (lane < ghost_start + REACH)
    ghosts = sheared(lead, trail, last)
    cells = [jnp.where(ghost_lane, g, c) for g, c in zip(ghosts, cells)]
    section = strip_section(cells, flows_ref, cells_ref, layers)
    lead, trail = [], []
    for f in range(FIELDS):
        flows_ref[f, SUB : SUB + height] = section[f]
        lead.append(flows_ref[f, SUB + REACH : SUB + REACH + rows])
        trail.append(flows_ref[f, SUB + REACH + 1 : SUB + REACH + 1 + rows])
    ghosts = sheared(lead, trail, jnp.logical_not(last))
    lane = lax.rem(lanes_of((rows, cols)), 2 * RIGHT)
    for part in range(2):
        total = jnp.zeros((rows, cols), jnp.float32)
        for i in range(4):
            inside = (lane >= i * PACK) & (lane < (i + 1) * PACK)
            total = jnp.where(inside, move(ghosts[4 * part + i], i * PACK - REACH), total)
        packed[part] = total


def section_tiles(cells_ref, flow_y, flow_z, partial, tiles, emit):
    _, layers, rows, cols = cells_ref.shape
    lane = lanes_of((SUB, cols))
    weights = layer_weights(layers)
    for z in range(layers):
        for t in range(rows // SUB):
            span = pl.ds(t * SUB, SUB)
            cells = [cells_ref[f, z, span, :] for f in range(FIELDS)]
            velocity, pressure = primitives(cells)
            flows = flux(cells, velocity, pressure, 1)
            for f in range(FIELDS):
                if flows[f] is not None:
                    flow_y[f, z, span, :] = flows[f]
            if t not in tiles:
                continue
            flows = flux(cells, velocity, pressure, 2)
            for f in range(FIELDS):
                if flows[f] is not None:
                    flow_z[f, z, span, :] = flows[f]
            flows = flux(cells, velocity, pressure, 0)
            for f in range(FIELDS):
                partial[f, z, span, :] = along_lanes(cells[f], flows[f], lane, 0.0, 0.0)
    for z in range(layers):
        for t in tiles:
            start = t * SUB
            for f in range(FIELDS):

                def near(ref, layer, shift, f=f, start=start):
                    return ref[f, layer, pl.ds(start + shift, SUB), :]

                cells = near(cells_ref, z, 0)
                total = partial[f, z, pl.ds(start, SUB), :]
                around = near(cells_ref, z, 1) + near(cells_ref, z, -1)
                around = around + near(cells_ref, (z + 1) % layers, 0) + near(cells_ref, (z - 1) % layers, 0)
                total = total + viscosity * (around - 6.0 * cells)
                if f != 5:
                    for distance, weight in stencil:
                        total = total - weight * (near(flow_y, z, distance) - near(flow_y, z, -distance))
                if f != 6:
                    for distance, weight in weights.items():
                        total = total - weight * near(flow_z, (z + distance) % layers, 0)
                emit(f, z, t, cells + time_step * total)


def end_terms(halo, layers):
    lane = lax.rem(lanes_of(halo[0].shape), halo[0].shape[-1] // layers)
    low, high = (lane >= REACH) & (lane < 2 * REACH), (lane >= 2 * REACH) & (lane < 3 * REACH)
    velocity, pressure = primitives(halo)
    flows = flux(halo, velocity, pressure, 0)
    result = []
    for f in range(FIELDS):
        up, down = move(halo[f], 1), move(halo[f], -1)
        from_low = jnp.where(lane < 2 * REACH + 1, viscosity * up, 0.0)
        from_high = jnp.where(lane >= 2 * REACH - 1, viscosity * down, 0.0)
        if flows[f] is not None:
            for distance, weight in stencil:
                from_low = from_low + jnp.where(lane < 2 * REACH + distance, weight * move(flows[f], distance), 0.0)
                from_high = from_high - jnp.where(lane >= 2 * REACH - distance, weight * move(flows[f], -distance), 0.0)
        result.append(jnp.where(high, from_low, jnp.where(low, from_high, 0.0)))
    return result


def to_plane(strip, z, layers):
    return move(strip, -(z * (strip.shape[-1] // layers) + 2 * REACH))


def ends_strip(left, right, lane):
    return jnp.where(lane < 2 * REACH, left, right)


def first_kernel(state, first, second, section, cells_ref, flow_y, flow_z, partial):
    odd_az, _, _ = axis_place("az")
    _, layers, rows, _ = state.shape
    even = odd_az == 0
    width = 2 * REACH
    for f in range(FIELDS):
        for z in range(layers):
            place = slice((f * layers + z) * width, (f * layers + z + 1) * width)
            before, after = neighbours(first[place, :], second[place, :], even)
            cells_ref[f, z, 2 * SUB - width : 2 * SUB, :] = before
            cells_ref[f, z, 2 * SUB : 2 * SUB + rows, :] = state[f, z]
            cells_ref[f, z, 2 * SUB + rows : 2 * SUB + rows + width, :] = after

    def emit(f, z, t, value):
        section[f, z, (t - 1) * SUB : t * SUB, :] = value

    section_tiles(cells_ref, flow_y, flow_z, partial, range(1, 3 + rows // SUB), emit)


def ends_kernel(shifts, state, own, first, second, halo, partial, section, strips, window, flows_ref, strip_ref, *, wrap):
    odd_az, _, _ = axis_place("az")
    _, begins, last = axis_place("rad")
    _, layers, rows, cols = state.shape
    slot = cols // layers
    height = rows + 2 * SUB
    even = odd_az == 0
    fill_window(window, own, first, second, even)
    shift = shifts[0, 0]
    begin = jnp.where(last, rows - 1 - shift + wrap * rows, rows + shift - wrap * rows)
    lead = split_pairs([window[t, pl.ds(begin, height), :] for t in range(own.shape[0])])
    trail = split_pairs([window[t, pl.ds(begin + 1, height), :] for t in range(own.shape[0])])
    ghosts = sheared(lead, trail, begins)
    lane = lax.rem(lanes_of((height, cols)), slot)
    whole = lanes_of((rows, cols))
    own_lane = ((lane >= 2 * REACH) & (lane < 3 * REACH)) | ((lane >= RIGHT) & (lane < RIGHT + REACH))
    blank = jnp.zeros((SUB, cols), jnp.float32)
    strip_cells, beyond = [], []
    for f in range(FIELDS):
        corner = first.shape[0] - FIELDS + f
        before, after = neighbours(first[corner], second[corner], even)
        strip = jnp.concatenate([before, halo[f], after], axis=0)
        own_part = jnp.zeros((rows, cols), jnp.float32)
        for z in range(layers):
            low = z * slot + 2 * REACH
            own_part = jnp.where((whole >= low) & (whole < low + REACH), move(state[f, z], low), own_part)
            low = z * slot + RIGHT
            own_part = jnp.where((whole >= low) & (whole < low + REACH), move(state[f, z], low + REACH), own_part)
        own_part = jnp.concatenate([blank, own_part, blank], axis=0)
        strip_cells.append(jnp.where(own_lane, own_part, strip))
        right = move(strip, 2 * REACH - RIGHT - REACH)
        left = jnp.where(begins, ghosts[f], strip)
        right = jnp.where(last, move(ghosts[f], REACH), right)
        beyond.append(ends_strip(left, right, lane))
    terms = end_terms(beyond, layers)
    column = lanes_of((height, cols))
    ends = (column < REACH) | (column >= cols - REACH)
    for f in range(FIELDS):
        for z in range(layers):
            added = jnp.where(ends, time_step * to_plane(terms[f], z, layers), 0.0)
            section[f, z] = partial[f, z] + added
    done = strip_section(strip_cells, flows_ref, strip_ref, layers)
    for f in range(FIELDS):
        right = move(done[f], 2 * REACH - RIGHT - REACH)
        strips[f] = ends_strip(done[f], right, lane)[SUB : SUB + rows]


def second_kernel(state, section, result, flow_y, flow_z, partial):
    _, _, rows, _ = state.shape

    def emit(f, z, t, value):
        rows_of = slice((t - 1) * SUB, t * SUB)
        result[f, z, rows_of, :] = 0.5 * state[f, z, rows_of, :] + 0.5 * value

    section_tiles(section, flow_y, flow_z, partial, range(1, 1 + rows // SUB), emit)


def last_kernel(partial, strips, packed, result):
    _, begins, last = axis_place("rad")
    _, layers, rows, cols = partial.shape
    lane = lax.rem(lanes_of((rows, cols)), cols // layers)
    halo = []
    for f in range(FIELDS):
        ghosts = packed[f // 4]
        left = jnp.where(begins, move(ghosts, REACH - (f % 4) * PACK), strips[f])
        right = jnp.where(last, move(ghosts, 2 * REACH - (f % 4) * PACK), strips[f])
        halo.append(ends_strip(left, right, lane))
    terms = end_terms(halo, layers)
    column = lanes_of((rows, cols))
    ends = (column < REACH) | (column >= cols - REACH)
    for f in range(FIELDS):
        for z in range(layers):
            added = jnp.where(ends, 0.5 * time_step * to_plane(terms[f], z, layers), 0.0)
            result[f, z] = partial[f, z] + added


VMEM = pl.BlockSpec(memory_space=pltpu.VMEM)
SMEM = pl.BlockSpec(memory_space=pltpu.SMEM)
HBM = pl.BlockSpec(memory_space=pltpu.HBM)


BIG = 63 * 2**20


def call(kernel, name, outs, *args, scratch=(), flops=0, smem=0, hbm=0, sems=0, out_spec=VMEM, limit=24 * 2**20, cost=2**18):
    many = isinstance(outs, list)
    scratch_shapes = [pltpu.VMEM(shape, jnp.float32) for shape in scratch]
    if sems:
        scratch_shapes.append(pltpu.SemaphoreType.DMA((sems,)))
    return pl.pallas_call(
        kernel,
        name=name,
        out_shape=outs,
        in_specs=[SMEM] * smem + [HBM] * hbm + [VMEM] * (len(args) - smem - hbm),
        out_specs=[out_spec] * len(outs) if many else out_spec,
        scratch_shapes=scratch_shapes,
        compiler_params=pltpu.CompilerParams(vmem_limit_bytes=limit),
        cost_estimate=pl.CostEstimate(flops=flops, bytes_accessed=cost, transcendentals=0),
    )(*args)


def routes(az_count, rad_count, wrap, turn):
    def listed(target):
        pairs = []
        for a in range(az_count):
            for r in range(rad_count):
                to_a, to_r = target(a, r)
                pairs.append((a * rad_count + r, (to_a % az_count) * rad_count + to_r))
        return pairs

    end = rad_count - 1

    def near(a, r):
        if r == 0:
            return a + wrap, end
        if r == end:
            return a - wrap, 0
        return a, r + 1 if r % 2 else r - 1

    def half_turn(a, r):
        extra = -turn if r == 0 else turn if r == end else 0
        return a + az_count // 2 + extra, r

    return (
        listed(near),
        listed(lambda a, r: (a, r ^ 1)),
        listed(lambda a, r: (a ^ 1, r)),
        listed(lambda a, r: (((a + 1) ^ 1) - 1, r)),
        listed(half_turn),
    )


def exchange_and_step(wrap, turned_wrap, shifts, state, near, far, pairs, *bulks):
    _, layers, rows, cols = state.shape
    turn = turned_wrap - wrap
    near_route, far_route, first_route, second_route, turn_route = routes(
        lax.axis_size("az"), lax.axis_size("rad"), wrap, turn
    )
    axes = ("az", "rad")
    far_in = lax.ppermute(far, axes, far_route)
    near_in = lax.ppermute(near, axes, near_route)
    bulks = [lax.ppermute(part, axes, (first_route, second_route)[i]) for i, part in enumerate(bulks)]
    parcel = struct(4 * rows // SUB + FIELDS, SUB, cols)
    own, halo, for_first, for_second = call(
        join_kernel,
        "join",
        [struct(4, rows, cols), struct(FIELDS, rows, cols), parcel, parcel],
        pairs,
        near_in,
        far_in,
    )
    first = lax.ppermute(for_first, axes, first_route)
    second = lax.ppermute(for_second, axes, second_route)
    height = rows + 2 * SUB
    padded = (FIELDS, layers, height + 2 * SUB, cols)
    partial = call(
        first_kernel,
        "first_section",
        struct(FIELDS, layers, height, cols),
        state,
        *bulks,
        scratch=[padded] * 4,
    )
    window = (4, 3 * rows + 2 * SUB, cols)
    packed = call(
        functools.partial(far_kernel, turn=turn, wrap=turned_wrap),
        "far",
        struct(2, rows, cols),
        shifts,
        own,
        first,
        second,
        partial,
        scratch=[window] + [(FIELDS, rows + 3 * SUB, cols)] * 2,
    )
    packed = lax.ppermute(packed, axes, turn_route)
    section, strips = call(
        functools.partial(ends_kernel, wrap=wrap),
        "first_ends",
        [struct(FIELDS, layers, height, cols), struct(FIELDS, rows, cols)],
        shifts,
        state,
        own,
        first,
        second,
        halo,
        partial,
        scratch=[window] + [(FIELDS, height + 2 * SUB, cols)] * 2,
    )
    partial = call(
        second_kernel,
        "second_section",
        struct(FIELDS, layers, rows, cols),
        state,
        section,
        scratch=[(FIELDS, layers, height, cols)] * 3,
    )
    return call(last_kernel, "second_ends", struct(FIELDS, layers, rows, cols), partial, strips, packed)


def shards(density, momentum, magnetic, tracer, offsets):
    layers, rows, cols = density.shape
    state, near, far, pairs, index, shifts, *bulks = pl.pallas_call(
        edges_kernel,
        name="edges",
        out_shape=[
            struct(FIELDS, layers, rows, cols),
            struct(4, rows, cols),
            struct(6, rows, cols),
            struct(4, rows, cols),
            jax.ShapeDtypeStruct((1,), jnp.int32),
            jax.ShapeDtypeStruct((SUB, cols), jnp.int32),
        ]
        + [struct(FIELDS * layers * 2 * REACH, cols)] * 2,
        in_specs=[HBM] * 5,
        out_specs=[VMEM] * 4 + [HBM] + [VMEM] * 3,
        scratch_shapes=[pltpu.SMEM((2,), jnp.int32), pltpu.SMEM((1,), jnp.int32), pltpu.SemaphoreType.DMA((6,))],
        compiler_params=pltpu.CompilerParams(vmem_limit_bytes=BIG),
    )(density, momentum, magnetic, tracer, offsets)
    branches = [
        functools.partial(exchange_and_step, wrap, turned_wrap) for wrap in range(2) for turned_wrap in range(2)
    ]
    return lax.switch(index[0], branches, shifts, state, near, far, pairs, *bulks)


def solution(mesh):
    placed = (
        P(None, "az", "rad"),
        P(None, None, "az", "rad"),
        P(None, None, "az", "rad"),
        P(None, "az", "rad"),
        P(),
    )
    return jax.shard_map(
        shards, mesh=mesh, in_specs=placed, out_specs=P(None, None, "az", "rad"), check_vma=False
    )
```

```python
import functools

import jax
import jax.numpy as jnp
from jax import lax
from jax.experimental import pallas as pl
from jax.experimental.pallas import tpu as pltpu
from jax.sharding import PartitionSpec as P

time_step = 0.025
viscosity = 0.5
sound_squared = 1.0
shear_speed = 1.0
frac_weight = 0.375
stencil = ((1, 45.0 / 60.0), (2, -9.0 / 60.0), (3, 1.0 / 60.0))
REACH = 3
FIELDS = 8
SUB = 8
RIGHT = 16
PACK = 8


def struct(*shape):
    return jax.ShapeDtypeStruct(shape, jnp.float32)


def lanes_of(shape):
    return lax.broadcasted_iota(jnp.int32, shape, len(shape) - 1)


def move(values, by):
    count = values.shape[-1]
    if isinstance(by, int):
        by = by % count
        return values if by == 0 else pltpu.roll(values, by, values.ndim - 1)
    return pltpu.roll(values, lax.rem(by + count, count), values.ndim - 1)


def primitives(cells):
    inverse = 1.0 / cells[0]
    velocity = [cells[1 + i] * inverse for i in range(3)]
    squares = cells[4] * cells[4] + cells[5] * cells[5] + cells[6] * cells[6]
    return velocity, sound_squared * cells[0] + 0.5 * squares


def flux(cells, velocity, pressure, direction):
    speed, normal = velocity[direction], cells[4 + direction]
    result = [cells[1 + direction]]
    for i in range(3):
        term = cells[1 + i] * speed - cells[4 + i] * normal
        result.append(term + pressure if i == direction else term)
    for i in range(3):
        result.append(None if i == direction else speed * cells[4 + i] - normal * velocity[i])
    result.append(cells[7] * speed)
    return result


def along_lanes(values, flows, lane, halo_values=None, halo_flows=None):
    count = values.shape[-1]

    def ends(array, halo, width):
        if halo is None:
            return array, array
        return jnp.where(lane < width, halo, array), jnp.where(lane >= count - width, halo, array)

    above, below = ends(values, halo_values, 1)
    up, down = viscosity * above, viscosity * below
    if flows is None:
        return move(up, -1) + move(down, 1)
    total = None
    for distance, weight in stencil:
        above, below = ends(flows, halo_flows, distance)
        plus, minus = -weight * above, weight * below
        if distance == 1:
            plus, minus = plus + up, minus + down
        pair = move(plus, -distance) + move(minus, distance)
        total = pair if total is None else total + pair
    return total


def layer_weights(layers):
    folded = {}
    for distance, weight in stencil:
        for signed, share in ((distance, weight), (-distance, -weight)):
            folded[signed % layers] = folded.get(signed % layers, 0.0) + share
    return {distance: weight for distance, weight in folded.items() if weight != 0.0 and distance != 0}


def strip_section(cells, flows_ref, cells_ref, layers):
    rows, count = cells[0].shape
    slot = count // layers
    velocity, pressure = primitives(cells)
    flow_x, flow_y, flow_z = (flux(cells, velocity, pressure, d) for d in range(3))
    weights = layer_weights(layers)
    result = []
    for f in range(FIELDS):
        cells_ref[f, SUB : SUB + rows] = cells[f]
        if flow_y[f] is not None:
            flows_ref[f, SUB : SUB + rows] = flow_y[f]
    for f in range(FIELDS):
        total = along_lanes(cells[f], flow_x[f], None)
        total = total + viscosity * (move(cells[f], slot) + move(cells[f], -slot))
        if flow_z[f] is not None:
            for distance, weight in weights.items():
                total = total - weight * move(flow_z[f], -distance * slot)
        total = total + viscosity * (cells_ref[f, SUB - 1 : SUB - 1 + rows] + cells_ref[f, SUB + 1 : SUB + 1 + rows])
        if flow_y[f] is not None:
            for distance, weight in stencil:
                total = total - weight * (
                    flows_ref[f, SUB + distance : SUB + distance + rows]
                    - flows_ref[f, SUB - distance : SUB - distance + rows]
                )
        total = total - 6.0 * viscosity * cells[f]
        result.append(cells[f] + time_step * total)
    return result


def sheared(lead, trail, inner):
    first = jnp.where(inner, 1.0 - frac_weight, frac_weight)
    jump = jnp.where(inner, shear_speed, -shear_speed)
    ghosts = [first * a + (1.0 - first) * b for a, b in zip(lead, trail)]
    ghosts[2] = ghosts[2] + jump * ghosts[0]
    return ghosts


def split_pairs(pairs):
    return [pairs[f // 2] if f % 2 == 0 else move(pairs[f // 2], -RIGHT) for f in range(FIELDS)]


def fill_window(window_ref, own_ref, first_ref, second_ref, even):
    tiles, rows, _ = own_ref.shape
    parts = rows // SUB
    for t in range(tiles):
        window_ref[t, SUB + rows : SUB + 2 * rows] = own_ref[t]
        for i in range(parts):
            before, after = neighbours(first_ref[t * parts + i], second_ref[t * parts + i], even)
            window_ref[t, SUB + i * SUB : SUB + (i + 1) * SUB] = before
            window_ref[t, SUB + 2 * rows + i * SUB : SUB + 2 * rows + (i + 1) * SUB] = after


def neighbours(first, second, even):
    return jnp.where(even, second, first), jnp.where(even, first, second)


def axis_place(axis):
    place = lax.axis_index(axis)
    return lax.rem(place, 2), place == 0, place == lax.axis_size(axis) - 1


def rows_for(rows):
    odd, _, _ = axis_place("az")
    return pl.multiple_of((1 - odd) * (rows - SUB), SUB), pl.multiple_of(odd * (rows - SUB), SUB)


def edges_kernel(density, momentum, magnetic, tracer, offsets, state, near, far, pairs, index, shifts, *rest):
    *bulks, held, sems = rest
    layers, rows, cols = density.shape
    slot = cols // layers
    parts = (
        (density, state.at[0]),
        (momentum, state.at[1:4]),
        (magnetic, state.at[4:7]),
        (tracer, state.at[7]),
        (offsets, held),
    )
    copies = [pltpu.make_async_copy(source, target, sems.at[i]) for i, (source, target) in enumerate(parts)]
    for copy in copies:
        copy.start()
    copies[4].wait()
    half = rows * lax.axis_size("az") // 2
    index[0] = jnp.where(held[0] > rows - 4, 2, 0) + jnp.where(held[1] > rows - 4 + half, 1, 0)
    for i in range(2):
        shifts[i : i + 1, :] = jnp.full((1, cols), held[i])
    odd, _, last = axis_place("rad")
    lane = lanes_of((rows, cols))
    width = 2 * REACH
    near_parts, far_parts = [jnp.zeros((rows, cols), jnp.float32)] * 2, [jnp.zeros((rows, cols), jnp.float32)] * 2
    pair_parts = [jnp.zeros((rows, cols), jnp.float32)] * 4
    shift_pair = jnp.where(last, REACH, width)
    for f in range(FIELDS):
        if f in (0, 1, 4, 7):
            copies[(0, 1, 4, 7).index(f)].wait()
        for z in range(layers):
            plane = state[f, z]
            start = z * slot + (f % 4) * PACK
            inside = (lane >= start) & (lane < start + PACK)
            left, right = move(plane, start), move(plane, start + width)
            near_parts[f // 4] = jnp.where(inside, jnp.where(odd == 1, right, left), near_parts[f // 4])
            far_parts[f // 4] = jnp.where(inside, jnp.where(odd == 1, left, right), far_parts[f // 4])
            start = z * slot + (f % 2) * RIGHT
            begin = start + jnp.where(last, 0, width)
            inside = (lane >= begin) & (lane < begin + REACH)
            pair_parts[f // 2] = jnp.where(inside, move(plane, start + shift_pair), pair_parts[f // 2])
    for part in range(2):
        near[part], far[part] = near_parts[part], far_parts[part]
    for part in range(2, far.shape[0]):
        far[part] = jnp.zeros((rows, cols), jnp.float32)
    for part in range(2, near.shape[0]):
        near[part] = jnp.zeros((rows, cols), jnp.float32)
    for part in range(4):
        pairs[part] = pair_parts[part]
    odd_az, _, _ = axis_place("az")
    for f in range(FIELDS):
        for z in range(layers):
            head, tail = state[f, z, :width, :], state[f, z, rows - width :, :]
            place = slice((f * layers + z) * width, (f * layers + z + 1) * width)
            bulks[0][place, :] = jnp.where(odd_az == 1, head, tail)
            bulks[1][place, :] = jnp.where(odd_az == 1, tail, head)


def join_kernel(pairs, near, far, own, halo, first, second):
    odd, _, last = axis_place("rad")
    tiles, rows, cols = pairs.shape
    slot = 2 * RIGHT
    lane = lax.rem(lanes_of((rows, cols)), slot)
    offset = jnp.where(last, REACH, 0)
    parts = rows // SUB
    starts = rows_for(rows)
    for part in range(tiles):
        total = pairs[part]
        for f in (2 * part, 2 * part + 1):
            begin = (f % 2) * RIGHT + offset
            inside = (lane >= begin) & (lane < begin + 2 * REACH)
            total = jnp.where(inside, move(near[f // 4], begin - (f % 4) * PACK), total)
        own[part] = total
        for i in range(parts):
            first[part * parts + i] = second[part * parts + i] = total[i * SUB : (i + 1) * SUB]
    for f in range(FIELDS):
        a, b = far[f // 4], near[f // 4]
        left, right = jnp.where(odd == 1, a, b), jnp.where(odd == 1, b, a)
        left, right = move(left, -(f % 4) * PACK), move(right, RIGHT + REACH - (f % 4) * PACK)
        halo[f] = jnp.where(
            lane < 2 * REACH,
            left,
            jnp.where((lane >= RIGHT + REACH) & (lane < RIGHT + 3 * REACH), right, 0.0),
        )
        for out, start in zip((first, second), starts):
            out[tiles * parts + f] = halo[f, pl.ds(start, SUB), :]


def far_kernel(offsets, own, first, second, _, packed, window, flows_ref, cells_ref, *, turn, wrap):
    odd_az, _, _ = axis_place("az")
    _, _, last = axis_place("rad")
    tiles, rows, cols = own.shape
    layers = cols // (2 * RIGHT)
    total_rows = rows * lax.axis_size("az")
    fill_window(window, own, first, second, odd_az == 0)
    shift, turned = offsets[0, 0], offsets[1, 0] - total_rows // 2
    height = rows + SUB
    base = SUB + rows
    begin = jnp.where(last, base - REACH - 1 - turned + wrap * rows, base - REACH + turned - wrap * rows)
    edge = jnp.where(
        last, base - REACH - 1 - turned + turn * rows + shift, base - REACH + turned - turn * rows - shift - 1
    )
    cells = split_pairs([window[t, pl.ds(begin, height), :] for t in range(tiles)])
    lead = split_pairs([window[t, pl.ds(edge, height), :] for t in range(tiles)])
    trail = split_pairs([window[t, pl.ds(edge + 1, height), :] for t in range(tiles)])
    lane = lax.rem(lanes_of((height, cols)), 2 * RIGHT)
    ghost_start = jnp.where(last, 0, 2 * REACH)
    ghost_lane = (lane >= ghost_start) & (lane < ghost_start + REACH)
    ghosts = sheared(lead, trail, last)
    cells = [jnp.where(ghost_lane, g, c) for g, c in zip(ghosts, cells)]
    section = strip_section(cells, flows_ref, cells_ref, layers)
    lead, trail = [], []
    for f in range(FIELDS):
        flows_ref[f, SUB : SUB + height] = section[f]
        lead.append(flows_ref[f, SUB + REACH : SUB + REACH + rows])
        trail.append(flows_ref[f, SUB + REACH + 1 : SUB + REACH + 1 + rows])
    ghosts = sheared(lead, trail, jnp.logical_not(last))
    lane = lax.rem(lanes_of((rows, cols)), 2 * RIGHT)
    for part in range(2):
        total = jnp.zeros((rows, cols), jnp.float32)
        for i in range(4):
            inside = (lane >= i * PACK) & (lane < (i + 1) * PACK)
            total = jnp.where(inside, move(ghosts[4 * part + i], i * PACK - REACH), total)
        packed[part] = total


def section_tiles(cells_ref, flow_y, flow_z, partial, tiles, emit):
    _, layers, rows, cols = cells_ref.shape
    lane = lanes_of((SUB, cols))
    weights = layer_weights(layers)
    for z in range(layers):
        for t in range(rows // SUB):
            span = pl.ds(t * SUB, SUB)
            cells = [cells_ref[f, z, span, :] for f in range(FIELDS)]
            velocity, pressure = primitives(cells)
            flows = flux(cells, velocity, pressure, 1)
            for f in range(FIELDS):
                if flows[f] is not None:
                    flow_y[f, z, span, :] = flows[f]
            if t not in tiles:
                continue
            flows = flux(cells, velocity, pressure, 2)
            for f in range(FIELDS):
                if flows[f] is not None:
                    flow_z[f, z, span, :] = flows[f]
            flows = flux(cells, velocity, pressure, 0)
            for f in range(FIELDS):
                partial[f, z, span, :] = along_lanes(cells[f], flows[f], lane, 0.0, 0.0)
    for z in range(layers):
        for t in tiles:
            start = t * SUB
            for f in range(FIELDS):

                def near(ref, layer, shift, f=f, start=start):
                    return ref[f, layer, pl.ds(start + shift, SUB), :]

                cells = near(cells_ref, z, 0)
                total = partial[f, z, pl.ds(start, SUB), :]
                around = near(cells_ref, z, 1) + near(cells_ref, z, -1)
                around = around + near(cells_ref, (z + 1) % layers, 0) + near(cells_ref, (z - 1) % layers, 0)
                total = total + viscosity * (around - 6.0 * cells)
                if f != 5:
                    for distance, weight in stencil:
                        total = total - weight * (near(flow_y, z, distance) - near(flow_y, z, -distance))
                if f != 6:
                    for distance, weight in weights.items():
                        total = total - weight * near(flow_z, (z + distance) % layers, 0)
                emit(f, z, t, cells + time_step * total)


def end_terms(halo, layers):
    lane = lax.rem(lanes_of(halo[0].shape), halo[0].shape[-1] // layers)
    low, high = (lane >= REACH) & (lane < 2 * REACH), (lane >= 2 * REACH) & (lane < 3 * REACH)
    velocity, pressure = primitives(halo)
    flows = flux(halo, velocity, pressure, 0)
    result = []
    for f in range(FIELDS):
        up, down = move(halo[f], 1), move(halo[f], -1)
        from_low = jnp.where(lane < 2 * REACH + 1, viscosity * up, 0.0)
        from_high = jnp.where(lane >= 2 * REACH - 1, viscosity * down, 0.0)
        if flows[f] is not None:
            for distance, weight in stencil:
                from_low = from_low + jnp.where(lane < 2 * REACH + distance, weight * move(flows[f], distance), 0.0)
                from_high = from_high - jnp.where(lane >= 2 * REACH - distance, weight * move(flows[f], -distance), 0.0)
        result.append(jnp.where(high, from_low, jnp.where(low, from_high, 0.0)))
    return result


def to_plane(strip, z, layers):
    return move(strip, -(z * (strip.shape[-1] // layers) + 2 * REACH))


def ends_strip(left, right, lane):
    return jnp.where(lane < 2 * REACH, left, right)


def first_kernel(state, first, second, section, cells_ref, flow_y, flow_z, partial):
    odd_az, _, _ = axis_place("az")
    _, layers, rows, _ = state.shape
    even = odd_az == 0
    width = 2 * REACH
    for f in range(FIELDS):
        for z in range(layers):
            place = slice((f * layers + z) * width, (f * layers + z + 1) * width)
            before, after = neighbours(first[place, :], second[place, :], even)
            cells_ref[f, z, 2 * SUB - width : 2 * SUB, :] = before
            cells_ref[f, z, 2 * SUB : 2 * SUB + rows, :] = state[f, z]
            cells_ref[f, z, 2 * SUB + rows : 2 * SUB + rows + width, :] = after

    def emit(f, z, t, value):
        section[f, z, (t - 1) * SUB : t * SUB, :] = value

    section_tiles(cells_ref, flow_y, flow_z, partial, range(1, 3 + rows // SUB), emit)


def ends_kernel(shifts, state, own, first, second, halo, partial, section, strips, window, flows_ref, strip_ref, *, wrap):
    odd_az, _, _ = axis_place("az")
    _, begins, last = axis_place("rad")
    _, layers, rows, cols = state.shape
    slot = cols // layers
    height = rows + 2 * SUB
    even = odd_az == 0
    fill_window(window, own, first, second, even)
    shift = shifts[0, 0]
    begin = jnp.where(last, rows - 1 - shift + wrap * rows, rows + shift - wrap * rows)
    lead = split_pairs([window[t, pl.ds(begin, height), :] for t in range(own.shape[0])])
    trail = split_pairs([window[t, pl.ds(begin + 1, height), :] for t in range(own.shape[0])])
    ghosts = sheared(lead, trail, begins)
    lane = lax.rem(lanes_of((height, cols)), slot)
    whole = lanes_of((rows, cols))
    own_lane = ((lane >= 2 * REACH) & (lane < 3 * REACH)) | ((lane >= RIGHT) & (lane < RIGHT + REACH))
    blank = jnp.zeros((SUB, cols), jnp.float32)
    strip_cells, beyond = [], []
    for f in range(FIELDS):
        corner = first.shape[0] - FIELDS + f
        before, after = neighbours(first[corner], second[corner], even)
        strip = jnp.concatenate([before, halo[f], after], axis=0)
        own_part = jnp.zeros((rows, cols), jnp.float32)
        for z in range(layers):
            low = z * slot + 2 * REACH
            own_part = jnp.where((whole >= low) & (whole < low + REACH), move(state[f, z], low), own_part)
            low = z * slot + RIGHT
            own_part = jnp.where((whole >= low) & (whole < low + REACH), move(state[f, z], low + REACH), own_part)
        own_part = jnp.concatenate([blank, own_part, blank], axis=0)
        strip_cells.append(jnp.where(own_lane, own_part, strip))
        right = move(strip, 2 * REACH - RIGHT - REACH)
        left = jnp.where(begins, ghosts[f], strip)
        right = jnp.where(last, move(ghosts[f], REACH), right)
        beyond.append(ends_strip(left, right, lane))
    terms = end_terms(beyond, layers)
    column = lanes_of((height, cols))
    ends = (column < REACH) | (column >= cols - REACH)
    for f in range(FIELDS):
        for z in range(layers):
            added = jnp.where(ends, time_step * to_plane(terms[f], z, layers), 0.0)
            section[f, z] = partial[f, z] + added
    done = strip_section(strip_cells, flows_ref, strip_ref, layers)
    for f in range(FIELDS):
        right = move(done[f], 2 * REACH - RIGHT - REACH)
        strips[f] = ends_strip(done[f], right, lane)[SUB : SUB + rows]


def second_kernel(state, section, result, flow_y, flow_z, partial):
    _, _, rows, _ = state.shape

    def emit(f, z, t, value):
        rows_of = slice((t - 1) * SUB, t * SUB)
        result[f, z, rows_of, :] = 0.5 * state[f, z, rows_of, :] + 0.5 * value

    section_tiles(section, flow_y, flow_z, partial, range(1, 1 + rows // SUB), emit)


def last_kernel(partial, strips, packed, result):
    _, begins, last = axis_place("rad")
    _, layers, rows, cols = partial.shape
    lane = lax.rem(lanes_of((rows, cols)), cols // layers)
    halo = []
    for f in range(FIELDS):
        ghosts = packed[f // 4]
        left = jnp.where(begins, move(ghosts, REACH - (f % 4) * PACK), strips[f])
        right = jnp.where(last, move(ghosts, 2 * REACH - (f % 4) * PACK), strips[f])
        halo.append(ends_strip(left, right, lane))
    terms = end_terms(halo, layers)
    column = lanes_of((rows, cols))
    ends = (column < REACH) | (column >= cols - REACH)
    for f in range(FIELDS):
        for z in range(layers):
            added = jnp.where(ends, 0.5 * time_step * to_plane(terms[f], z, layers), 0.0)
            result[f, z] = partial[f, z] + added


VMEM = pl.BlockSpec(memory_space=pltpu.VMEM)
SMEM = pl.BlockSpec(memory_space=pltpu.SMEM)
HBM = pl.BlockSpec(memory_space=pltpu.HBM)


BIG = 63 * 2**20


def call(kernel, name, outs, *args, scratch=(), flops=0, smem=0, hbm=0, sems=0, out_spec=VMEM, limit=24 * 2**20, cost=2**18):
    many = isinstance(outs, list)
    scratch_shapes = [pltpu.VMEM(shape, jnp.float32) for shape in scratch]
    if sems:
        scratch_shapes.append(pltpu.SemaphoreType.DMA((sems,)))
    return pl.pallas_call(
        kernel,
        name=name,
        out_shape=outs,
        in_specs=[SMEM] * smem + [HBM] * hbm + [VMEM] * (len(args) - smem - hbm),
        out_specs=[out_spec] * len(outs) if many else out_spec,
        scratch_shapes=scratch_shapes,
        compiler_params=pltpu.CompilerParams(vmem_limit_bytes=limit),
        cost_estimate=pl.CostEstimate(flops=flops, bytes_accessed=cost, transcendentals=0),
    )(*args)


def routes(az_count, rad_count, wrap, turn):
    def listed(target):
        pairs = []
        for a in range(az_count):
            for r in range(rad_count):
                to_a, to_r = target(a, r)
                pairs.append((a * rad_count + r, (to_a % az_count) * rad_count + to_r))
        return pairs

    end = rad_count - 1

    def near(a, r):
        if r == 0:
            return a + wrap, end
        if r == end:
            return a - wrap, 0
        return a, r + 1 if r % 2 else r - 1

    def half_turn(a, r):
        extra = -turn if r == 0 else turn if r == end else 0
        return a + az_count // 2 + extra, r

    return (
        listed(near),
        listed(lambda a, r: (a, r ^ 1)),
        listed(lambda a, r: (a ^ 1, r)),
        listed(lambda a, r: (((a + 1) ^ 1) - 1, r)),
        listed(half_turn),
    )


def exchange_and_step(wrap, turned_wrap, shifts, state, near, far, pairs, *bulks):
    _, layers, rows, cols = state.shape
    turn = turned_wrap - wrap
    near_route, far_route, first_route, second_route, turn_route = routes(
        lax.axis_size("az"), lax.axis_size("rad"), wrap, turn
    )
    axes = ("az", "rad")
    far_in = lax.ppermute(far, axes, far_route)
    near_in = lax.ppermute(near, axes, near_route)
    bulks = [lax.ppermute(part, axes, (first_route, second_route)[i]) for i, part in enumerate(bulks)]
    parcel = struct(4 * rows // SUB + FIELDS, SUB, cols)
    own, halo, for_first, for_second = call(
        join_kernel,
        "join",
        [struct(4, rows, cols), struct(FIELDS, rows, cols), parcel, parcel],
        pairs,
        near_in,
        far_in,
    )
    first = lax.ppermute(for_first, axes, first_route)
    second = lax.ppermute(for_second, axes, second_route)
    height = rows + 2 * SUB
    padded = (FIELDS, layers, height + 2 * SUB, cols)
    partial = call(
        first_kernel,
        "first_section",
        struct(FIELDS, layers, height, cols),
        state,
        *bulks,
        scratch=[padded] * 4,
    )
    window = (4, 3 * rows + 2 * SUB, cols)
    packed = call(
        functools.partial(far_kernel, turn=turn, wrap=turned_wrap),
        "far",
        struct(2, rows, cols),
        shifts,
        own,
        first,
        second,
        partial,
        scratch=[window] + [(FIELDS, rows + 3 * SUB, cols)] * 2,
    )
    packed = lax.ppermute(packed, axes, turn_route)
    section, strips = call(
        functools.partial(ends_kernel, wrap=wrap),
        "first_ends",
        [struct(FIELDS, layers, height, cols), struct(FIELDS, rows, cols)],
        shifts,
        state,
        own,
        first,
        second,
        halo,
        partial,
        scratch=[window] + [(FIELDS, height + 2 * SUB, cols)] * 2,
    )
    partial = call(
        second_kernel,
        "second_section",
        struct(FIELDS, layers, rows, cols),
        state,
        section,
        scratch=[(FIELDS, layers, height, cols)] * 3,
    )
    return call(last_kernel, "second_ends", struct(FIELDS, layers, rows, cols), partial, strips, packed)


def shards(density, momentum, magnetic, tracer, offsets):
    layers, rows, cols = density.shape
    state, near, far, pairs, index, shifts, *bulks = pl.pallas_call(
        edges_kernel,
        name="edges",
        out_shape=[
            struct(FIELDS, layers, rows, cols),
            struct(4, rows, cols),
            struct(6, rows, cols),
            struct(4, rows, cols),
            pltpu.SMEM((1,), jnp.int32),
            jax.ShapeDtypeStruct((SUB, cols), jnp.int32),
        ]
        + [struct(FIELDS * layers * 2 * REACH, cols)] * 2,
        in_specs=[HBM] * 5,
        out_specs=[VMEM] * 4 + [SMEM] + [VMEM] * 3,
        scratch_shapes=[pltpu.SMEM((2,), jnp.int32), pltpu.SemaphoreType.DMA((5,))],
        compiler_params=pltpu.CompilerParams(vmem_limit_bytes=BIG),
    )(density, momentum, magnetic, tracer, offsets)
    branches = [
        functools.partial(exchange_and_step, wrap, turned_wrap) for wrap in range(2) for turned_wrap in range(2)
    ]
    return lax.switch(index[0], branches, shifts, state, near, far, pairs, *bulks)


def solution(mesh):
    placed = (
        P(None, "az", "rad"),
        P(None, None, "az", "rad"),
        P(None, None, "az", "rad"),
        P(None, "az", "rad"),
        P(),
    )
    return jax.shard_map(
        shards, mesh=mesh, in_specs=placed, out_specs=P(None, None, "az", "rad"), check_vma=False
    )
```

```python
import functools

import jax
import jax.numpy as jnp
from jax import lax
from jax.experimental import pallas as pl
from jax.experimental.pallas import tpu as pltpu
from jax.sharding import PartitionSpec as P

time_step = 0.025
viscosity = 0.5
sound_squared = 1.0
shear_speed = 1.0
frac_weight = 0.375
stencil = ((1, 45.0 / 60.0), (2, -9.0 / 60.0), (3, 1.0 / 60.0))
REACH = 3
FIELDS = 8
SUB = 8
RIGHT = 16
PACK = 8


def struct(*shape):
    return jax.ShapeDtypeStruct(shape, jnp.float32)


def lanes_of(shape):
    return lax.broadcasted_iota(jnp.int32, shape, len(shape) - 1)


def move(values, by):
    count = values.shape[-1]
    if isinstance(by, int):
        by = by % count
        return values if by == 0 else pltpu.roll(values, by, values.ndim - 1)
    return pltpu.roll(values, lax.rem(by + count, count), values.ndim - 1)


def primitives(cells):
    inverse = 1.0 / cells[0]
    velocity = [cells[1 + i] * inverse for i in range(3)]
    squares = cells[4] * cells[4] + cells[5] * cells[5] + cells[6] * cells[6]
    return velocity, sound_squared * cells[0] + 0.5 * squares


def flux(cells, velocity, pressure, direction):
    speed, normal = velocity[direction], cells[4 + direction]
    result = [cells[1 + direction]]
    for i in range(3):
        term = cells[1 + i] * speed - cells[4 + i] * normal
        result.append(term + pressure if i == direction else term)
    for i in range(3):
        result.append(None if i == direction else speed * cells[4 + i] - normal * velocity[i])
    result.append(cells[7] * speed)
    return result


def along_lanes(values, flows, lane, halo_values=None, halo_flows=None):
    count = values.shape[-1]

    def ends(array, halo, width):
        if halo is None:
            return array, array
        return jnp.where(lane < width, halo, array), jnp.where(lane >= count - width, halo, array)

    above, below = ends(values, halo_values, 1)
    up, down = viscosity * above, viscosity * below
    if flows is None:
        return move(up, -1) + move(down, 1)
    total = None
    for distance, weight in stencil:
        above, below = ends(flows, halo_flows, distance)
        plus, minus = -weight * above, weight * below
        if distance == 1:
            plus, minus = plus + up, minus + down
        pair = move(plus, -distance) + move(minus, distance)
        total = pair if total is None else total + pair
    return total


def layer_weights(layers):
    folded = {}
    for distance, weight in stencil:
        for signed, share in ((distance, weight), (-distance, -weight)):
            folded[signed % layers] = folded.get(signed % layers, 0.0) + share
    return {distance: weight for distance, weight in folded.items() if weight != 0.0 and distance != 0}


def strip_section(cells, flows_ref, cells_ref, layers):
    rows, count = cells[0].shape
    slot = count // layers
    velocity, pressure = primitives(cells)
    flow_x, flow_y, flow_z = (flux(cells, velocity, pressure, d) for d in range(3))
    weights = layer_weights(layers)
    result = []
    for f in range(FIELDS):
        cells_ref[f, SUB : SUB + rows] = cells[f]
        if flow_y[f] is not None:
            flows_ref[f, SUB : SUB + rows] = flow_y[f]
    for f in range(FIELDS):
        total = along_lanes(cells[f], flow_x[f], None)
        total = total + viscosity * (move(cells[f], slot) + move(cells[f], -slot))
        if flow_z[f] is not None:
            for distance, weight in weights.items():
                total = total - weight * move(flow_z[f], -distance * slot)
        total = total + viscosity * (cells_ref[f, SUB - 1 : SUB - 1 + rows] + cells_ref[f, SUB + 1 : SUB + 1 + rows])
        if flow_y[f] is not None:
            for distance, weight in stencil:
                total = total - weight * (
                    flows_ref[f, SUB + distance : SUB + distance + rows]
                    - flows_ref[f, SUB - distance : SUB - distance + rows]
                )
        total = total - 6.0 * viscosity * cells[f]
        result.append(cells[f] + time_step * total)
    return result


def sheared(lead, trail, inner):
    first = jnp.where(inner, 1.0 - frac_weight, frac_weight)
    jump = jnp.where(inner, shear_speed, -shear_speed)
    ghosts = [first * a + (1.0 - first) * b for a, b in zip(lead, trail)]
    ghosts[2] = ghosts[2] + jump * ghosts[0]
    return ghosts


def split_pairs(pairs):
    return [pairs[f // 2] if f % 2 == 0 else move(pairs[f // 2], -RIGHT) for f in range(FIELDS)]


def fill_window(window_ref, own_ref, first_ref, second_ref, even):
    tiles, rows, _ = own_ref.shape
    parts = rows // SUB
    for t in range(tiles):
        window_ref[t, SUB + rows : SUB + 2 * rows] = own_ref[t]
        for i in range(parts):
            before, after = neighbours(first_ref[t * parts + i], second_ref[t * parts + i], even)
            window_ref[t, SUB + i * SUB : SUB + (i + 1) * SUB] = before
            window_ref[t, SUB + 2 * rows + i * SUB : SUB + 2 * rows + (i + 1) * SUB] = after


def neighbours(first, second, even):
    return jnp.where(even, second, first), jnp.where(even, first, second)


def axis_place(axis):
    place = lax.axis_index(axis)
    return lax.rem(place, 2), place == 0, place == lax.axis_size(axis) - 1


def rows_for(rows):
    odd, _, _ = axis_place("az")
    return pl.multiple_of((1 - odd) * (rows - SUB), SUB), pl.multiple_of(odd * (rows - SUB), SUB)


def edges_kernel(density, momentum, magnetic, tracer, offsets, state, near, far, pairs, index, shifts, *rest):
    *bulks, held, sems = rest
    layers, rows, cols = density.shape
    slot = cols // layers
    parts = (
        (density, state.at[0]),
        (momentum, state.at[1:4]),
        (magnetic, state.at[4:7]),
        (tracer, state.at[7]),
        (offsets, held),
    )
    copies = [pltpu.make_async_copy(source, target, sems.at[i]) for i, (source, target) in enumerate(parts)]
    for copy in copies:
        copy.start()
    copies[4].wait()
    half = rows * lax.axis_size("az") // 2
    index[0] = jnp.where(held[0] > rows - 4, 2, 0) + jnp.where(held[1] > rows - 4 + half, 1, 0)
    for i in range(2):
        shifts[i : i + 1, :] = jnp.full((1, cols), held[i])
    odd, _, last = axis_place("rad")
    lane = lanes_of((rows, cols))
    width = 2 * REACH
    near_parts, far_parts = [jnp.zeros((rows, cols), jnp.float32)] * 2, [jnp.zeros((rows, cols), jnp.float32)] * 2
    pair_parts = [jnp.zeros((rows, cols), jnp.float32)] * 4
    shift_pair = jnp.where(last, REACH, width)
    for f in range(FIELDS):
        if f in (0, 1, 4, 7):
            copies[(0, 1, 4, 7).index(f)].wait()
        for z in range(layers):
            plane = state[f, z]
            start = z * slot + (f % 4) * PACK
            inside = (lane >= start) & (lane < start + PACK)
            left, right = move(plane, start), move(plane, start + width)
            near_parts[f // 4] = jnp.where(inside, jnp.where(odd == 1, right, left), near_parts[f // 4])
            far_parts[f // 4] = jnp.where(inside, jnp.where(odd == 1, left, right), far_parts[f // 4])
            start = z * slot + (f % 2) * RIGHT
            begin = start + jnp.where(last, 0, width)
            inside = (lane >= begin) & (lane < begin + REACH)
            pair_parts[f // 2] = jnp.where(inside, move(plane, start + shift_pair), pair_parts[f // 2])
    for part in range(2):
        near[part], far[part] = near_parts[part], far_parts[part]
    for part in range(2, far.shape[0]):
        far[part] = jnp.zeros((rows, cols), jnp.float32)
    for part in range(2, near.shape[0]):
        near[part] = jnp.zeros((rows, cols), jnp.float32)
    for part in range(4):
        pairs[part] = pair_parts[part]
    odd_az, _, _ = axis_place("az")
    for f in range(FIELDS):
        for z in range(layers):
            head, tail = state[f, z, :width, :], state[f, z, rows - width :, :]
            place = slice((f * layers + z) * width, (f * layers + z + 1) * width)
            bulks[0][place, :] = jnp.where(odd_az == 1, head, tail)
            bulks[1][place, :] = jnp.where(odd_az == 1, tail, head)


def join_kernel(pairs, near, far, own, halo, first, second):
    odd, _, last = axis_place("rad")
    tiles, rows, cols = pairs.shape
    slot = 2 * RIGHT
    lane = lax.rem(lanes_of((rows, cols)), slot)
    offset = jnp.where(last, REACH, 0)
    parts = rows // SUB
    starts = rows_for(rows)
    for part in range(tiles):
        total = pairs[part]
        for f in (2 * part, 2 * part + 1):
            begin = (f % 2) * RIGHT + offset
            inside = (lane >= begin) & (lane < begin + 2 * REACH)
            total = jnp.where(inside, move(near[f // 4], begin - (f % 4) * PACK), total)
        own[part] = total
        for i in range(parts):
            first[part * parts + i] = second[part * parts + i] = total[i * SUB : (i + 1) * SUB]
    for f in range(FIELDS):
        a, b = far[f // 4], near[f // 4]
        left, right = jnp.where(odd == 1, a, b), jnp.where(odd == 1, b, a)
        left, right = move(left, -(f % 4) * PACK), move(right, RIGHT + REACH - (f % 4) * PACK)
        halo[f] = jnp.where(
            lane < 2 * REACH,
            left,
            jnp.where((lane >= RIGHT + REACH) & (lane < RIGHT + 3 * REACH), right, 0.0),
        )
        for out, start in zip((first, second), starts):
            out[tiles * parts + f] = halo[f, pl.ds(start, SUB), :]


def far_kernel(offsets, own, first, second, _, packed, window, flows_ref, cells_ref, *, turn, wrap):
    odd_az, _, _ = axis_place("az")
    _, _, last = axis_place("rad")
    tiles, rows, cols = own.shape
    layers = cols // (2 * RIGHT)
    total_rows = rows * lax.axis_size("az")
    fill_window(window, own, first, second, odd_az == 0)
    shift, turned = offsets[0, 0], offsets[1, 0] - total_rows // 2
    height = rows + SUB
    base = SUB + rows
    begin = jnp.where(last, base - REACH - 1 - turned + wrap * rows, base - REACH + turned - wrap * rows)
    edge = jnp.where(
        last, base - REACH - 1 - turned + turn * rows + shift, base - REACH + turned - turn * rows - shift - 1
    )
    cells = split_pairs([window[t, pl.ds(begin, height), :] for t in range(tiles)])
    lead = split_pairs([window[t, pl.ds(edge, height), :] for t in range(tiles)])
    trail = split_pairs([window[t, pl.ds(edge + 1, height), :] for t in range(tiles)])
    lane = lax.rem(lanes_of((height, cols)), 2 * RIGHT)
    ghost_start = jnp.where(last, 0, 2 * REACH)
    ghost_lane = (lane >= ghost_start) & (lane < ghost_start + REACH)
    ghosts = sheared(lead, trail, last)
    cells = [jnp.where(ghost_lane, g, c) for g, c in zip(ghosts, cells)]
    section = strip_section(cells, flows_ref, cells_ref, layers)
    lead, trail = [], []
    for f in range(FIELDS):
        flows_ref[f, SUB : SUB + height] = section[f]
        lead.append(flows_ref[f, SUB + REACH : SUB + REACH + rows])
        trail.append(flows_ref[f, SUB + REACH + 1 : SUB + REACH + 1 + rows])
    ghosts = sheared(lead, trail, jnp.logical_not(last))
    lane = lax.rem(lanes_of((rows, cols)), 2 * RIGHT)
    for part in range(2):
        total = jnp.zeros((rows, cols), jnp.float32)
        for i in range(4):
            inside = (lane >= i * PACK) & (lane < (i + 1) * PACK)
            total = jnp.where(inside, move(ghosts[4 * part + i], i * PACK - REACH), total)
        packed[part] = total


def section_tiles(cells_ref, flow_y, flow_z, partial, tiles, emit):
    _, layers, rows, cols = cells_ref.shape
    lane = lanes_of((SUB, cols))
    weights = layer_weights(layers)
    for z in range(layers):
        for t in range(rows // SUB):
            span = pl.ds(t * SUB, SUB)
            cells = [cells_ref[f, z, span, :] for f in range(FIELDS)]
            velocity, pressure = primitives(cells)
            flows = flux(cells, velocity, pressure, 1)
            for f in range(FIELDS):
                if flows[f] is not None:
                    flow_y[f, z, span, :] = flows[f]
            if t not in tiles:
                continue
            flows = flux(cells, velocity, pressure, 2)
            for f in range(FIELDS):
                if flows[f] is not None:
                    flow_z[f, z, span, :] = flows[f]
            flows = flux(cells, velocity, pressure, 0)
            for f in range(FIELDS):
                partial[f, z, span, :] = along_lanes(cells[f], flows[f], lane, 0.0, 0.0)
    for z in range(layers):
        for t in tiles:
            start = t * SUB
            for f in range(FIELDS):

                def near(ref, layer, shift, f=f, start=start):
                    return ref[f, layer, pl.ds(start + shift, SUB), :]

                cells = near(cells_ref, z, 0)
                total = partial[f, z, pl.ds(start, SUB), :]
                around = near(cells_ref, z, 1) + near(cells_ref, z, -1)
                around = around + near(cells_ref, (z + 1) % layers, 0) + near(cells_ref, (z - 1) % layers, 0)
                total = total + viscosity * (around - 6.0 * cells)
                if f != 5:
                    for distance, weight in stencil:
                        total = total - weight * (near(flow_y, z, distance) - near(flow_y, z, -distance))
                if f != 6:
                    for distance, weight in weights.items():
                        total = total - weight * near(flow_z, (z + distance) % layers, 0)
                emit(f, z, t, cells + time_step * total)


def end_terms(halo, layers):
    lane = lax.rem(lanes_of(halo[0].shape), halo[0].shape[-1] // layers)
    low, high = (lane >= REACH) & (lane < 2 * REACH), (lane >= 2 * REACH) & (lane < 3 * REACH)
    velocity, pressure = primitives(halo)
    flows = flux(halo, velocity, pressure, 0)
    result = []
    for f in range(FIELDS):
        up, down = move(halo[f], 1), move(halo[f], -1)
        from_low = jnp.where(lane < 2 * REACH + 1, viscosity * up, 0.0)
        from_high = jnp.where(lane >= 2 * REACH - 1, viscosity * down, 0.0)
        if flows[f] is not None:
            for distance, weight in stencil:
                from_low = from_low + jnp.where(lane < 2 * REACH + distance, weight * move(flows[f], distance), 0.0)
                from_high = from_high - jnp.where(lane >= 2 * REACH - distance, weight * move(flows[f], -distance), 0.0)
        result.append(jnp.where(high, from_low, jnp.where(low, from_high, 0.0)))
    return result


def to_plane(strip, z, layers):
    return move(strip, -(z * (strip.shape[-1] // layers) + 2 * REACH))


def ends_strip(left, right, lane):
    return jnp.where(lane < 2 * REACH, left, right)


def first_kernel(state, first, second, section, cells_ref, flow_y, flow_z, partial):
    odd_az, _, _ = axis_place("az")
    _, layers, rows, _ = state.shape
    even = odd_az == 0
    width = 2 * REACH
    for f in range(FIELDS):
        for z in range(layers):
            place = slice((f * layers + z) * width, (f * layers + z + 1) * width)
            before, after = neighbours(first[place, :], second[place, :], even)
            cells_ref[f, z, 2 * SUB - width : 2 * SUB, :] = before
            cells_ref[f, z, 2 * SUB : 2 * SUB + rows, :] = state[f, z]
            cells_ref[f, z, 2 * SUB + rows : 2 * SUB + rows + width, :] = after

    def emit(f, z, t, value):
        section[f, z, (t - 1) * SUB : t * SUB, :] = value

    section_tiles(cells_ref, flow_y, flow_z, partial, range(1, 3 + rows // SUB), emit)


def ends_kernel(shifts, state, own, first, second, halo, partial, section, strips, window, flows_ref, strip_ref, *, wrap):
    odd_az, _, _ = axis_place("az")
    _, begins, last = axis_place("rad")
    _, layers, rows, cols = state.shape
    slot = cols // layers
    height = rows + 2 * SUB
    even = odd_az == 0
    fill_window(window, own, first, second, even)
    shift = shifts[0, 0]
    begin = jnp.where(last, rows - 1 - shift + wrap * rows, rows + shift - wrap * rows)
    lead = split_pairs([window[t, pl.ds(begin, height), :] for t in range(own.shape[0])])
    trail = split_pairs([window[t, pl.ds(begin + 1, height), :] for t in range(own.shape[0])])
    ghosts = sheared(lead, trail, begins)
    lane = lax.rem(lanes_of((height, cols)), slot)
    whole = lanes_of((rows, cols))
    own_lane = ((lane >= 2 * REACH) & (lane < 3 * REACH)) | ((lane >= RIGHT) & (lane < RIGHT + REACH))
    blank = jnp.zeros((SUB, cols), jnp.float32)
    strip_cells, beyond = [], []
    for f in range(FIELDS):
        corner = first.shape[0] - FIELDS + f
        before, after = neighbours(first[corner], second[corner], even)
        strip = jnp.concatenate([before, halo[f], after], axis=0)
        own_part = jnp.zeros((rows, cols), jnp.float32)
        for z in range(layers):
            low = z * slot + 2 * REACH
            own_part = jnp.where((whole >= low) & (whole < low + REACH), move(state[f, z], low), own_part)
            low = z * slot + RIGHT
            own_part = jnp.where((whole >= low) & (whole < low + REACH), move(state[f, z], low + REACH), own_part)
        own_part = jnp.concatenate([blank, own_part, blank], axis=0)
        strip_cells.append(jnp.where(own_lane, own_part, strip))
        right = move(strip, 2 * REACH - RIGHT - REACH)
        left = jnp.where(begins, ghosts[f], strip)
        right = jnp.where(last, move(ghosts[f], REACH), right)
        beyond.append(ends_strip(left, right, lane))
    terms = end_terms(beyond, layers)
    column = lanes_of((height, cols))
    ends = (column < REACH) | (column >= cols - REACH)
    for f in range(FIELDS):
        for z in range(layers):
            added = jnp.where(ends, time_step * to_plane(terms[f], z, layers), 0.0)
            section[f, z] = partial[f, z] + added
    done = strip_section(strip_cells, flows_ref, strip_ref, layers)
    for f in range(FIELDS):
        right = move(done[f], 2 * REACH - RIGHT - REACH)
        strips[f] = ends_strip(done[f], right, lane)[SUB : SUB + rows]


def second_kernel(state, section, result, flow_y, flow_z, partial):
    _, _, rows, _ = state.shape

    def emit(f, z, t, value):
        rows_of = slice((t - 1) * SUB, t * SUB)
        result[f, z, rows_of, :] = 0.5 * state[f, z, rows_of, :] + 0.5 * value

    section_tiles(section, flow_y, flow_z, partial, range(1, 1 + rows // SUB), emit)


def terms_kernel(strips, packed, terms):
    _, begins, last = axis_place("rad")
    _, rows, cols = strips.shape
    lane = lax.rem(lanes_of((rows, cols)), 2 * RIGHT)
    halo = []
    for f in range(FIELDS):
        ghosts = packed[f // 4]
        left = jnp.where(begins, move(ghosts, REACH - (f % 4) * PACK), strips[f])
        right = jnp.where(last, move(ghosts, 2 * REACH - (f % 4) * PACK), strips[f])
        halo.append(ends_strip(left, right, lane))
    for f, term in enumerate(end_terms(halo, cols // (2 * RIGHT))):
        terms[f] = 0.5 * time_step * term


def last_kernel(partial, terms, result, final, sems):
    _, layers, rows, cols = partial.shape
    column = lanes_of((rows, cols))
    ends = (column < REACH) | (column >= cols - REACH)
    copies = []
    for f in range(FIELDS):
        for z in range(layers):
            final[f, z] = partial[f, z] + jnp.where(ends, to_plane(terms[f], z, layers), 0.0)
        copies.append(pltpu.make_async_copy(final.at[f], result.at[f], sems.at[f]))
        copies[f].start()
    for copy in copies:
        copy.wait()


VMEM = pl.BlockSpec(memory_space=pltpu.VMEM)
SMEM = pl.BlockSpec(memory_space=pltpu.SMEM)
HBM = pl.BlockSpec(memory_space=pltpu.HBM)


BIG = 63 * 2**20


def call(kernel, name, outs, *args, scratch=(), flops=0, smem=0, hbm=0, sems=0, out_spec=VMEM, limit=24 * 2**20, cost=2**18):
    many = isinstance(outs, list)
    scratch_shapes = [pltpu.VMEM(shape, jnp.float32) for shape in scratch]
    if sems:
        scratch_shapes.append(pltpu.SemaphoreType.DMA((sems,)))
    return pl.pallas_call(
        kernel,
        name=name,
        out_shape=outs,
        in_specs=[SMEM] * smem + [HBM] * hbm + [VMEM] * (len(args) - smem - hbm),
        out_specs=[out_spec] * len(outs) if many else out_spec,
        scratch_shapes=scratch_shapes,
        compiler_params=pltpu.CompilerParams(vmem_limit_bytes=limit),
        cost_estimate=pl.CostEstimate(flops=flops, bytes_accessed=cost, transcendentals=0),
    )(*args)


def routes(az_count, rad_count, wrap, turn):
    def listed(target):
        pairs = []
        for a in range(az_count):
            for r in range(rad_count):
                to_a, to_r = target(a, r)
                pairs.append((a * rad_count + r, (to_a % az_count) * rad_count + to_r))
        return pairs

    end = rad_count - 1

    def near(a, r):
        if r == 0:
            return a + wrap, end
        if r == end:
            return a - wrap, 0
        return a, r + 1 if r % 2 else r - 1

    def half_turn(a, r):
        extra = -turn if r == 0 else turn if r == end else 0
        return a + az_count // 2 + extra, r

    return (
        listed(near),
        listed(lambda a, r: (a, r ^ 1)),
        listed(lambda a, r: (a ^ 1, r)),
        listed(lambda a, r: (((a + 1) ^ 1) - 1, r)),
        listed(half_turn),
    )


def exchange_and_step(wrap, turned_wrap, shifts, state, near, far, pairs, *bulks):
    _, layers, rows, cols = state.shape
    turn = turned_wrap - wrap
    near_route, far_route, first_route, second_route, turn_route = routes(
        lax.axis_size("az"), lax.axis_size("rad"), wrap, turn
    )
    axes = ("az", "rad")
    far_in = lax.ppermute(far, axes, far_route)
    near_in = lax.ppermute(near, axes, near_route)
    bulks = [lax.ppermute(part, axes, (first_route, second_route)[i]) for i, part in enumerate(bulks)]
    parcel = struct(4 * rows // SUB + FIELDS, SUB, cols)
    own, halo, for_first, for_second = call(
        join_kernel,
        "join",
        [struct(4, rows, cols), struct(FIELDS, rows, cols), parcel, parcel],
        pairs,
        near_in,
        far_in,
    )
    first = lax.ppermute(for_first, axes, first_route)
    second = lax.ppermute(for_second, axes, second_route)
    height = rows + 2 * SUB
    padded = (FIELDS, layers, height + 2 * SUB, cols)
    partial = call(
        first_kernel,
        "first_section",
        struct(FIELDS, layers, height, cols),
        state,
        *bulks,
        scratch=[padded] * 4,
    )
    window = (4, 3 * rows + 2 * SUB, cols)
    packed = call(
        functools.partial(far_kernel, turn=turn, wrap=turned_wrap),
        "far",
        struct(2, rows, cols),
        shifts,
        own,
        first,
        second,
        partial,
        scratch=[window] + [(FIELDS, rows + 3 * SUB, cols)] * 2,
    )
    packed = lax.ppermute(packed, axes, turn_route)
    section, strips = call(
        functools.partial(ends_kernel, wrap=wrap),
        "first_ends",
        [struct(FIELDS, layers, height, cols), struct(FIELDS, rows, cols)],
        shifts,
        state,
        own,
        first,
        second,
        halo,
        partial,
        scratch=[window] + [(FIELDS, height + 2 * SUB, cols)] * 2,
    )
    partial = call(
        second_kernel,
        "second_section",
        struct(FIELDS, layers, rows, cols),
        state,
        section,
        scratch=[(FIELDS, layers, height, cols)] * 3,
    )
    return partial, call(terms_kernel, "second_terms", struct(FIELDS, rows, cols), strips, packed)


def shards(density, momentum, magnetic, tracer, offsets):
    layers, rows, cols = density.shape
    state, near, far, pairs, index, shifts, *bulks = pl.pallas_call(
        edges_kernel,
        name="edges",
        out_shape=[
            struct(FIELDS, layers, rows, cols),
            struct(4, rows, cols),
            struct(6, rows, cols),
            struct(4, rows, cols),
            pltpu.SMEM((1,), jnp.int32),
            jax.ShapeDtypeStruct((SUB, cols), jnp.int32),
        ]
        + [struct(FIELDS * layers * 2 * REACH, cols)] * 2,
        in_specs=[HBM] * 5,
        out_specs=[VMEM] * 4 + [SMEM] + [VMEM] * 3,
        scratch_shapes=[pltpu.SMEM((2,), jnp.int32), pltpu.SemaphoreType.DMA((5,))],
        compiler_params=pltpu.CompilerParams(vmem_limit_bytes=BIG),
    )(density, momentum, magnetic, tracer, offsets)
    branches = [
        functools.partial(exchange_and_step, wrap, turned_wrap) for wrap in range(2) for turned_wrap in range(2)
    ]
    partial, terms = lax.switch(index[0], branches, shifts, state, near, far, pairs, *bulks)
    return call(
        last_kernel,
        "second_ends",
        struct(FIELDS, layers, rows, cols),
        partial,
        terms,
        scratch=[(FIELDS, layers, rows, cols)],
        sems=FIELDS,
        out_spec=HBM,
    )


def solution(mesh):
    placed = (
        P(None, "az", "rad"),
        P(None, None, "az", "rad"),
        P(None, None, "az", "rad"),
        P(None, "az", "rad"),
        P(),
    )
    return jax.shard_map(
        shards, mesh=mesh, in_specs=placed, out_specs=P(None, None, "az", "rad"), check_vma=False
    )
```
